512 devices in a mesh: group: 16 (over y, core), dev: 32 (over x, z).
Axes of the slice: x: 4, y: 8, z: 8, core: 2. Of those that a mesh axis runs over, the one named last changes fastest.
Arguments:
- coarse_temp: float32 [128, 512, 128], P('group', 'dev'), may hold values from 0.5 to 1.5
- coarse_cond: float32 [128, 512, 128], P('group', 'dev'), may hold values from 0.25 to 1
- routes: int32 [16, 32, 8, 16, 1], P('group', 'dev'), may hold values from 0 to 31; in each aligned block of 128 rows (0 to 127, 128 to 255, ..., all dimensions but the last counted through in order) at most 6 rows name the same one
- track_start: int32 [16, 32, 8, 16], P('group', 'dev'), may hold values from 0 to 127
- track_depth: int32 [16, 32, 8, 16], P('group', 'dev'), may hold values from 2 to 64
- power: float32 [16, 32, 8, 16], P('group', 'dev'), may hold values from 0.2 to 1
- fine_temp: float32 [16, 32, 32, 6, 4, 256], P('group', 'dev'), may hold values from 0.5 to 1.5
- fine_strain: float32 [16, 32, 32, 6, 4, 256], P('group', 'dev'), may hold values from -1 to 1
Outputs:
- coarse_next: float32 [128, 512, 128], P('group', 'dev')
- fine_temp_next: float32 [16, 32, 32, 6, 4, 256], P('group', 'dev')
- fine_strain_next: float32 [16, 32, 32, 6, 4, 256], P('group', 'dev')
The draws below stay inside these ranges and needn't reach their ends.
Inputs may be any that keep to these rules, and one draw needn't show every extreme that they name: `routes`: among the coarse columns of one device, no owner is named more than 6 times, a bound that some block reaches; every owner is named by some column of the group.
All inputs are finite; a program needn't handle non-finite values.
Results may differ from the reference program's by a relative error of at most 0.0003.
Values sent between devices are 32-bit elements; how exact they have to be, the bound alone decides.
A program may use at most 64 MiB of HBM per device.

```python
import math
import jax
import jax.numpy as jnp
import numpy as np
from jax import lax

CX = 8
CY = 16
NZ = 128
NX = 128
NY = 512
CAP = 6
N_GROUP = 16
N_DEV = 32


def place_ends(drawn, rng, low, largest):
    index_at = [jax.random.randint(jax.random.fold_in(rng, axis), (), 0, length) for axis, length in enumerate(drawn.shape)]
    longest = drawn.shape.index(max(drawn.shape))
    next_to = index_at[:longest] + [(index_at[longest] + 1) % drawn.shape[longest]] + index_at[longest + 1:]
    return drawn.at[tuple(index_at)].set(low).at[tuple(next_to)].set(largest)


def shard_levels(rng, shape, shards, smallest, top_value):
    gain, own = 1.0, jax.random.fold_in(rng, 6)
    for dim, shards_of in shards:
        steps = jnp.exp(jax.random.uniform(jax.random.fold_in(own, dim), (shards_of,), jnp.float32, smallest / len(shards), top_value / len(shards)))
        gain = gain * jnp.repeat(steps, shape[dim] // shards_of).reshape([-1 if axis == dim else 1 for axis in range(len(shape))])
    return gain


def deal_out(key, own, number, rows, number_of, top, most, slope):
    sequence = jax.random.permutation(key, number_of)
    crowded, ordinary = portions_of(number_of, rows * top, most, slope, True), portions_of(number_of, rows * top, most, slope, False)
    places = jnp.arange(number_of)

    def named(tallies, turn):
        used = int((tallies > 0).sum())
        fixed = max(1, used // 4)
        shifted = fixed + (places - fixed + turn * (used - fixed)) % max(1, number_of - fixed)
        return jnp.zeros((number_of,), jnp.int32).at[sequence[jnp.where(places < fixed, places, shifted)]].set(jnp.asarray(tallies, jnp.int32))

    tallies = jnp.where(number % 4 == 0, named(crowded, number // 4), named(ordinary, number - number // 4 - 1))
    mixed = jax.random.permutation(jax.random.fold_in(own, 3), number_of)
    giver, sink = mixed[0:number_of // 2 * 2:2], mixed[1:number_of // 2 * 2:2]
    room = jnp.minimum(tallies[giver] - 1, most - tallies[sink]) // 2
    room = jnp.where((giver == sequence[0]) | (sink == sequence[0]) | (tallies[sink] == 0), 0, jnp.maximum(room, 0))
    shifted = jax.random.randint(jax.random.fold_in(own, 4), (number_of // 2,), 0, 1 << 20) % (room + 1)
    tallies = tallies.at[giver].add(-shifted).at[sink].add(shifted)
    items = jnp.searchsorted(jnp.cumsum(tallies), jnp.arange(rows * top), side="right").astype(jnp.int32)
    listing = items.reshape(top, rows).T
    listing = listing[jax.random.permutation(jax.random.fold_in(own, 1), rows)]
    turn = jax.random.randint(jax.random.fold_in(own, 2), (rows, 1), 0, top)
    return jnp.take_along_axis(listing, (jnp.arange(top)[None, :] + turn) % top, axis=1)


def portions_of(number_of, total, limit, slope, full):
    portions = [(1 << 20) // math.isqrt(rank ** slope) + 1 for rank in range(1, number_of + 1)]
    largest = limit if full else min(limit, max(-(-total // number_of), total * portions[0] // sum(portions)))
    least = 1 if total - largest >= number_of - 1 else 0
    counts, surplus = [largest] + [least] * (number_of - 1), total - largest - least * (number_of - 1)
    while surplus > 0:
        candidates = [i for i in range(1, number_of) if counts[i] < largest] or [i for i in range(1, number_of) if counts[i] < limit]
        mass, budget = sum([portions[i] for i in candidates]), surplus
        for i in candidates:
            extra = min(limit - counts[i], max(1, budget * portions[i] // mass), surplus)
            counts[i] = counts[i] + extra
            surplus = surplus - extra
    return np.array(counts)


def normal_values(rng, extent, scale, most, split=(), held_as=jnp.bfloat16):
    gain = shard_levels(rng, extent, split, -0.22, 0.18) if split else 1.0
    values = jax.random.normal(rng, extent, jnp.float32) * scale * gain
    return jnp.minimum(jnp.maximum(values, -most), most).astype(held_as)


def setup_inputs(seed: int = 0) -> dict:
    arg_keys = jax.random.split(jax.random.key(seed), 9)
    coarse_temp = jnp.clip(0.5 + 1.0 * jax.random.uniform(arg_keys[0], (NX, NY, NZ), jnp.float32) ** shard_levels(arg_keys[0], (NX, NY, NZ), ((0, 16), (1, 32)), -0.2, 0.2), 0.5, 1.5)
    coarse_cond = jnp.clip(jnp.exp(math.log(1.0) - 1.3862944 * jax.random.uniform(arg_keys[1], (NX, NY, NZ), jnp.float32) ** shard_levels(arg_keys[1], (NX, NY, NZ), ((0, 16), (1, 32)), -0.2, 0.2)), 0.25, 1.0)
    routes_keys = jax.random.split(jax.random.fold_in(arg_keys[2], 1), N_GROUP * N_DEV * CX * CY // (CX * CY))
    routes_turns = jax.random.permutation(jax.random.fold_in(arg_keys[2], 3), N_GROUP * N_DEV * CX * CY // (CX * CY))
    routes = jax.vmap(lambda own, number: deal_out(jax.random.fold_in(arg_keys[2], 2), own, number, CX * CY, N_DEV, 1, CAP, 2))(routes_keys, routes_turns).reshape((N_GROUP, N_DEV, CX, CY, 1))
    track_start = place_ends(jax.random.randint(arg_keys[3], (N_GROUP, N_DEV, CX, CY), 0, NZ), jax.random.fold_in(arg_keys[3], 1), 0, NZ - 1).astype(jnp.int32)
    track_depth = place_ends(jax.random.randint(arg_keys[4], (N_GROUP, N_DEV, CX, CY), 2, NZ // 2 + 1), jax.random.fold_in(arg_keys[4], 1), 2, (NZ // 2 + 1) - 1).astype(jnp.int32)
    power = jnp.clip(jnp.exp(math.log(1.0) - 1.609438 * jax.random.uniform(arg_keys[5], (N_GROUP, N_DEV, CX, CY), jnp.float32) ** shard_levels(arg_keys[5], (N_GROUP, N_DEV, CX, CY), ((0, 16), (1, 32)), -0.2, 0.2)), 0.2, 1.0)
    fine_temp = jnp.clip(0.5 + 1.0 * jax.random.uniform(arg_keys[6], (N_GROUP, N_DEV, N_DEV, CAP, 4, 2 * NZ), jnp.float32) ** shard_levels(arg_keys[6], (N_GROUP, N_DEV, N_DEV, CAP, 4, 2 * NZ), ((0, 16), (1, 32)), -0.2, 0.2), 0.5, 1.5)
    fine_strain = normal_values(arg_keys[7], (N_GROUP, N_DEV, N_DEV, CAP, 4, 2 * NZ), 0.2, 1.0, ((0, 16), (1, 32)), jnp.float32)
    return {"coarse_temp": coarse_temp, "coarse_cond": coarse_cond, "routes": routes, "track_start": track_start, "track_depth": track_depth, "power": power, "fine_temp": fine_temp, "fine_strain": fine_strain}


R_COARSE = 0.08
R_FINE = 0.16
YIELD_BASE = 0.6
MELT_TEMP = 3.0
REF_TEMP = 1.0
YIELD_FLOOR = 0.05


def coarse_update(padded, conduct):
    zpad = jnp.pad(padded, ((0, 0), (0, 0), (1, 1)))
    center = zpad[1:-1, 1:-1, 1:-1]
    beside = zpad[2:, 1:-1, 1:-1] + zpad[:-2, 1:-1, 1:-1] + zpad[1:-1, 2:, 1:-1]
    beside = beside + zpad[1:-1, :-2, 1:-1] + zpad[1:-1, 1:-1, 2:] + zpad[1:-1, 1:-1, :-2]
    return center + R_COARSE * conduct * (beside - 6.0 * center)


def column_ghosts(old_pad, mid_pad):
    pieces = []
    for padded in (old_pad, mid_pad):
        pieces = pieces + [padded[:-2, 1:-1], padded[2:, 1:-1], padded[1:-1, :-2], padded[1:-1, 2:]]
    return jnp.stack(pieces, axis=2)


def owner_slots(owner_of, owner_count):
    one_hot = (owner_of[:, None] == jnp.arange(owner_count, dtype=jnp.int32)[None, :]).astype(jnp.int32)
    before = jnp.cumsum(one_hot, axis=0) - one_hot
    return jnp.sum(before * one_hot, axis=1).astype(jnp.int32)


def refine_z(values):
    return jnp.repeat(values, 2, axis=-1)


def fine_substep(thermal, strain, side_x, side_y, conduct_fine, source):
    above_cell = jnp.concatenate([thermal[..., 1:], jnp.zeros_like(thermal[..., :1])], axis=-1)
    below_cell = jnp.concatenate([jnp.zeros_like(thermal[..., :1]), thermal[..., :-1]], axis=-1)
    beside = jnp.flip(thermal, -3) + jnp.flip(thermal, -2) + side_x + side_y + above_cell + below_cell
    thermal = thermal + R_FINE * conduct_fine * (beside - 6.0 * thermal) + source
    stress = (REF_TEMP - thermal) - strain
    yield_limit = YIELD_BASE * jnp.maximum(1.0 - thermal / MELT_TEMP, YIELD_FLOOR)
    strain = strain + (stress - jnp.clip(stress, -yield_limit, yield_limit))
    return thermal, strain


def fine_advance(thermal, strain, ghosts, conduct, heat_rate, heat_start, heat_depth):
    depth_pos = jnp.arange(thermal.shape[-1], dtype=jnp.int32)
    inside = (depth_pos >= heat_start[..., None]) & (depth_pos < (heat_start + heat_depth)[..., None])
    source = jnp.where(inside, heat_rate[..., None], 0.0)[..., None, None, :]
    conduct_fine = refine_z(conduct)[..., None, None, :]
    for substep in range(2):
        side = refine_z(ghosts[..., 4 * substep:4 * substep + 4, :])
        side_x = side[..., 0:2, :][..., :, None, :]
        side_y = side[..., 2:4, :][..., None, :, :]
        thermal, strain = fine_substep(thermal, strain, side_x, side_y, conduct_fine, source)
    average = thermal.reshape(thermal.shape[:-3] + (4, thermal.shape[-1] // 2, 2)).mean(axis=(-3, -1))
    return thermal, strain, average


def by_device(values):
    values = values.reshape((CX, N_DEV, CY) + values.shape[2:])
    values = jnp.moveaxis(values, 1, 0)
    return values.reshape((N_DEV, CX * CY) + values.shape[3:])


def reference(coarse_temp, coarse_cond, routes, track_start, track_depth, power, fine_temp, fine_strain):
    old_pad = jnp.pad(coarse_temp, ((1, 1), (1, 1), (0, 0)))
    coarse_new = coarse_update(old_pad, coarse_cond)
    mid_pad = 0.5 * (old_pad + jnp.pad(coarse_new, ((1, 1), (1, 1), (0, 0))))
    row_count = CX * CY

    def per_group(group_index):
        offset = group_index * CX
        old_slab = lax.dynamic_slice_in_dim(old_pad, offset, CX + 2, 0)
        mid_slab = lax.dynamic_slice_in_dim(mid_pad, offset, CX + 2, 0)
        cond_slab = lax.dynamic_slice_in_dim(coarse_cond, offset, CX, 0)
        ghosts = by_device(column_ghosts(old_slab, mid_slab))
        conduct = by_device(cond_slab)
        owner_of = routes[group_index].reshape(N_DEV, row_count)
        slot_of = jax.vmap(lambda owners: owner_slots(owners, N_DEV))(owner_of)
        source_dev = jnp.broadcast_to(jnp.arange(N_DEV, dtype=jnp.int32)[:, None], owner_of.shape)
        temp_group = fine_temp[group_index]
        strain_group = fine_strain[group_index]
        thermal = temp_group[owner_of, source_dev, slot_of].reshape(N_DEV, row_count, 2, 2, 2 * NZ)
        strain = strain_group[owner_of, source_dev, slot_of].reshape(N_DEV, row_count, 2, 2, 2 * NZ)
        heat_rate = power[group_index].reshape(N_DEV, row_count)
        heat_start = track_start[group_index].reshape(N_DEV, row_count)
        heat_depth = track_depth[group_index].reshape(N_DEV, row_count)
        thermal, strain, average = fine_advance(thermal, strain, ghosts, conduct, heat_rate, heat_start, heat_depth)
        temp_out = jnp.zeros_like(temp_group).at[owner_of, source_dev, slot_of].set(thermal.reshape(N_DEV, row_count, 4, 2 * NZ))
        strain_out = jnp.zeros_like(strain_group).at[owner_of, source_dev, slot_of].set(strain.reshape(N_DEV, row_count, 4, 2 * NZ))
        coarse_part = jnp.moveaxis(average.reshape(N_DEV, CX, CY, NZ), 0, 1).reshape(CX, N_DEV * CY, NZ)
        return coarse_part, temp_out, strain_out

    coarse_parts, temp_next, strain_next = lax.map(per_group, jnp.arange(N_GROUP, dtype=jnp.int32))
    return coarse_parts.reshape(CX * N_GROUP, CY * N_DEV, NZ), temp_next, strain_next
```

```python
import functools

import jax
import jax.numpy as jnp
from jax import lax
from jax.experimental import pallas as pl
from jax.experimental.pallas import tpu as pltpu
from jax.sharding import PartitionSpec as P

R_COARSE = 0.08
R_FINE = 0.16
YIELD_BASE = 0.6
MELT_TEMP = 3.0
YIELD_FLOOR = 0.05

MESH = pl.DeviceIdType.MESH
F32 = jnp.float32
BF16 = jnp.bfloat16

X_CHIPS, Z_CHIPS = 4, 8
DEVS = X_CHIPS * Z_CHIPS
SLOTS = 6
COLS = DEVS * SLOTS
BX, BY, NZ = 8, 16, 128
ROWS = BX * BY

MEAN_AT = 0
COND_AT = 12
SCAL_AT = 18
GHOST_AT = 20
FIRST = 16
MSG = 56

CORNERS = ((1, 1), (1, -1), (-1, 1), (-1, -1))


def offset_of(step):
    pair = step // X_CHIPS
    return step % X_CHIPS, ((pair + 1) // 2) * (2 * (pair % 2) - 1)


def split(value):
    high = value.astype(BF16)
    return high, (value - high.astype(F32)).astype(BF16)


def pick(chooser, value, dims=((1,), (0,))):
    total = None
    for part in split(value):
        term = lax.dot_general(chooser, part, (dims, ((), ())), preferred_element_type=F32)
        total = term if total is None else total + term
    return total


def iota(shape, dim):
    return lax.broadcasted_iota(jnp.int32, shape, dim)


def kernel(
    par, ct, cc, ft, fs, cnew, tout, sout,
    outb, land, hys, hyl, hxs, hxl, hcs, hcl, oe, ce, me, field, side,
    hsend, hrecv, asend, arecv, bsend, brecv, lsem,
):
    group = lax.axis_index("group")
    groups = lax.axis_size("group")
    dev = lax.axis_index("dev")
    dx, dz = dev // Z_CHIPS, dev % Z_CHIPS

    def target(step):
        ox, oz = offset_of(step)
        return ((dx + ox) % X_CHIPS) * Z_CHIPS + (dz + oz + Z_CHIPS) % Z_CHIPS

    def origin(step):
        ox, oz = offset_of(step)
        return ((dx - ox + X_CHIPS) % X_CHIPS) * Z_CHIPS + (dz - oz + Z_CHIPS) % Z_CHIPS

    def near(dg, dd):
        return {"group": (group + dg + groups) % groups, "dev": (dev + dd + DEVS) % DEVS}

    barrier = pltpu.get_barrier_semaphore()

    def greet(step, carry):
        pl.semaphore_signal(barrier, inc=1, device_id={"dev": target(step)}, device_id_type=MESH)
        return carry

    lax.fori_loop(1, DEVS, greet, 0)
    for dg, dd in ((1, 0), (-1, 0)) + CORNERS:
        pl.semaphore_signal(barrier, inc=1, device_id=near(dg, dd), device_id_type=MESH)

    for x in range(BX):
        hys[0, 2 * x:2 * x + 2] = ct[x, BY - 2:BY]
        hys[0, 16 + x:17 + x] = cc[x, BY - 1:BY]
        hys[1, 2 * x:2 * x + 2] = ct[x, 0:2]
        hys[1, 16 + x:17 + x] = cc[x, 0:1]
    for i, (lo, edge) in enumerate(((BX - 2, BX - 1), (0, 0))):
        hxs[i, 0:16] = ct[lo]
        hxs[i, 16:32] = ct[lo + 1]
        hxs[i, 32:48] = cc[edge]
    for i, (dg, dd) in enumerate(CORNERS):
        row = BX - 1 if dg > 0 else 0
        hcs[i] = jnp.broadcast_to(ct[row, BY - 1:BY] if dd > 0 else ct[row, 0:1], (8, NZ))

    power, start, depth, owner = (par[i:i + 1] for i in range(4))
    owner_b = jnp.broadcast_to(owner, (DEVS, ROWS))
    hot = jnp.where(owner_b == iota((DEVS, ROWS), 0).astype(F32), 1.0, 0.0)
    earlier = jnp.where(iota((ROWS, ROWS), 0) < iota((ROWS, ROWS), 1), 1.0, 0.0).astype(BF16)
    before = lax.dot_general(hot.astype(BF16), earlier, (((1,), (0,)), ((), ())), preferred_element_type=F32)
    slot = jnp.sum(before * hot, axis=0, keepdims=True)
    code = slot * DEVS + owner
    to_slot = jnp.where(jnp.broadcast_to(code, (COLS, ROWS)) == iota((COLS, ROWS), 0).astype(F32), 1.0, 0.0).astype(BF16)
    code_t = jnp.transpose(jnp.broadcast_to(code, (ROWS, ROWS)))
    start_t = jnp.transpose(jnp.broadcast_to(start, (ROWS, ROWS)))
    depth_t = jnp.transpose(jnp.broadcast_to(depth, (ROWS, ROWS)))
    power_t = jnp.transpose(jnp.broadcast_to(power, (ROWS, ROWS)))
    lanes = iota((ROWS, ROWS), 1).astype(F32)
    from_slot = jnp.concatenate(
        [jnp.where(code_t == lanes, 1.0, 0.0), jnp.where(code_t == lanes + ROWS, 1.0, 0.0)], axis=1
    ).astype(BF16)

    conds = pick(to_slot, cc[...].reshape(ROWS, NZ))
    for k in range(SLOTS):
        outb[pl.ds(COND_AT + k, DEVS, stride=MSG), :] = conds[k * DEVS:(k + 1) * DEVS]
    at_slot = jnp.broadcast_to(slot, (8, ROWS)) == iota((8, ROWS), 0).astype(F32)
    blocks = [jnp.where(at_slot, jnp.broadcast_to(v, (8, ROWS)), 0.0) for v in (power, start, depth)]
    blocks = blocks + [jnp.where(at_slot, 1.0, 0.0), jnp.zeros((NZ - 32, ROWS), F32)]
    scalars = pick(hot.astype(BF16), jnp.concatenate(blocks, axis=0), ((1,), (1,)))
    outb[pl.ds(SCAL_AT, DEVS, stride=MSG), :] = scalars
    outb[pl.ds(SCAL_AT + 1, DEVS, stride=MSG), :] = jnp.zeros_like(scalars)

    for k in range(SLOTS):
        for half in range(2):
            total = None
            for ab in range(4):
                term = ft[pl.ds(8 * k + 4 * half + ab, DEVS, stride=8 * SLOTS), :]
                total = term if total is None else total + term
            outb[pl.ds(MEAN_AT + SLOTS * half + k, DEVS, stride=MSG), :] = 0.25 * total

    oe[...] = jnp.zeros_like(oe)
    ce[...] = jnp.zeros_like(ce)
    for x in range(BX):
        oe[2 + x, 8:24] = ct[x]
        ce[1 + x, 8:24] = cc[x]

    def own(lo, n):
        src = outb.at[pl.ds(pl.multiple_of(dev * MSG + lo, 8), n)]
        return pltpu.make_async_copy(src, land.at[dev, pl.ds(lo, n)], lsem)

    def message(peer, sender, lo, n, send, recv):
        src = outb.at[pl.ds(pl.multiple_of(peer * MSG + lo, 8), n)]
        return pltpu.make_async_remote_copy(
            src, land.at[sender, pl.ds(lo, n)], send.at[peer], recv.at[sender],
            device_id={"dev": peer}, device_id_type=MESH,
        )

    pl.semaphore_wait(barrier, DEVS - 1 + 2 + len(CORNERS))

    halos = []
    plan = [(hys, hyl, 0, 0, 1), (hys, hyl, 1, 0, -1), (hxs, hxl, 0, 1, 0), (hxs, hxl, 1, -1, 0)]
    plan = plan + [(hcs, hcl, i, dg, dd) for i, (dg, dd) in enumerate(CORNERS)]
    for number, (src, dst, i, dg, dd) in enumerate(plan):
        copy = pltpu.make_async_remote_copy(
            src.at[i], dst.at[i], hsend.at[number], hrecv.at[number],
            device_id=near(dg, dd), device_id_type=MESH,
        )
        copy.start()
        halos.append(copy)

    def send_first(step, carry):
        message(target(step), dev, 0, FIRST, asend, arecv).start()
        return carry

    lax.fori_loop(1, DEVS, send_first, 0)
    own_first = own(0, FIRST)
    own_first.start()

    for copy in halos:
        copy.wait_recv()

    low_x, high_x = group > 0, group < groups - 1
    low_y, high_y = dev > 0, dev < DEVS - 1

    def inside(ok, value):
        return jnp.where(ok, value, 0.0)

    for x in range(BX):
        oe[2 + x, 6:8] = inside(low_y, hyl[0, 2 * x:2 * x + 2])
        oe[2 + x, 24:26] = inside(high_y, hyl[1, 2 * x:2 * x + 2])
        ce[1 + x, 7:8] = inside(low_y, hyl[0, 16 + x:17 + x])
        ce[1 + x, 24:25] = inside(high_y, hyl[1, 16 + x:17 + x])
    oe[0, 8:24] = inside(low_x, hxl[0, 0:16])
    oe[1, 8:24] = inside(low_x, hxl[0, 16:32])
    ce[0, 8:24] = inside(low_x, hxl[0, 32:48])
    oe[BX + 2, 8:24] = inside(high_x, hxl[1, 0:16])
    oe[BX + 3, 8:24] = inside(high_x, hxl[1, 16:32])
    ce[BX + 1, 8:24] = inside(high_x, hxl[1, 32:48])
    oe[1, 7:8] = inside(low_x & low_y, hcl[0, 0:1])
    oe[1, 24:25] = inside(low_x & high_y, hcl[1, 0:1])
    oe[BX + 2, 7:8] = inside(high_x & low_y, hcl[2, 0:1])
    oe[BX + 2, 24:25] = inside(high_x & high_y, hcl[3, 0:1])

    lane = iota((32, NZ), 1)
    for x in range(BX + 2):
        cur = oe[x + 1]
        beside = oe[x] + oe[x + 2] + pltpu.roll(cur, 1, 0) + pltpu.roll(cur, 31, 0)
        beside = beside + jnp.where(lane == 0, 0.0, pltpu.roll(cur, 1, 1))
        beside = beside + jnp.where(lane == NZ - 1, 0.0, pltpu.roll(cur, NZ - 1, 1))
        new = cur + R_COARSE * ce[x] * (beside - 6.0 * cur)
        me[x] = 0.5 * (cur + new)

    for x in range(BX):
        for step, (arr, at) in enumerate(((oe, x + 2), (me, x + 1))):
            west, east = arr[at - 1, 8:24], arr[at + 1, 8:24]
            south, north = arr[at, 7:23], arr[at, 9:25]
            base, along_x, along_y = west + south, east - west, north - south
            for i, value in enumerate((base, along_x, along_y)):
                f = 3 * step + i
                field[x * BY:(x + 1) * BY, f * NZ:(f + 1) * NZ] = value
            side[step, x * BY:(x + 1) * BY] = base + 0.5 * (along_x + along_y)

    ghosts = pick(to_slot, field[...])
    for f in range(6):
        for k in range(SLOTS):
            outb[pl.ds(GHOST_AT + SLOTS * f + k, DEVS, stride=MSG), :] = ghosts[k * DEVS:(k + 1) * DEVS, f * NZ:(f + 1) * NZ]

    def send_rest(step, carry):
        message(target(step), dev, FIRST, MSG - FIRST, bsend, brecv).start()
        return carry

    lax.fori_loop(1, DEVS, send_rest, 0)
    own_first.wait()
    own_rest = own(FIRST, MSG - FIRST)
    own_rest.start()

    def take_first(step, carry):
        message(origin(step), origin(step), 0, FIRST, asend, arecv).wait_recv()
        return carry

    lax.fori_loop(1, DEVS, take_first, 0)
    halves = []
    for half in range(2):
        rows = [land[:, MEAN_AT + SLOTS * half + k, :] for k in range(SLOTS)] + [jnp.zeros((2 * ROWS - COLS, NZ), F32)]
        halves.append(jnp.concatenate(rows, axis=0))
    fine = pick(from_slot, jnp.concatenate(halves, axis=1))
    row_i, col_i = iota((2 * NZ, 2 * NZ), 0), iota((2 * NZ, 2 * NZ), 1)
    wanted = jnp.where(col_i < NZ, 2 * col_i, 2 * (col_i - NZ) + 1)
    high, low = split(fine)
    apart = jnp.where(row_i == wanted, 1.0, 0.0).astype(BF16)
    dims = (((1,), (0,)), ((), ()))
    both = lax.dot_general(high, apart, dims, preferred_element_type=F32)
    both = both + lax.dot_general(low, apart, dims, preferred_element_type=F32)
    even, odd = both[:, :NZ], both[:, NZ:]
    rate = R_FINE * cc[...].reshape(ROWS, NZ)
    place = iota((ROWS, NZ), 1)

    def heat(fine_cell):
        cell = fine_cell.astype(F32)
        return jnp.where((cell >= start_t) & (cell < start_t + depth_t), power_t, 0.0)

    heat_even, heat_odd = heat(2 * place), heat(2 * place + 1)
    for step in range(2):
        under = jnp.where(place == 0, 0.0, pltpu.roll(odd, 1, 1))
        over = jnp.where(place == NZ - 1, 0.0, pltpu.roll(even, NZ - 1, 1))
        ghost = side[step]
        even, odd = (
            even + rate * (ghost + odd + under - 4.0 * even) + heat_even,
            odd + rate * (ghost + even + over - 4.0 * odd) + heat_odd,
        )
    cnew[...] = (0.5 * (even + odd)).reshape(BX, BY, NZ)

    spread = jnp.where(iota((NZ, 2 * NZ), 1) // 2 == iota((NZ, 2 * NZ), 0), 1.0, 0.0).astype(BF16)
    cell = iota((SLOTS, 2 * NZ), 1)
    cell_f = cell.astype(F32)
    dims = (((1,), (0,)), ((), ()))

    def advance(peer):
        got = land[peer]
        high, low = split(got)
        wide = lax.dot_general(high, spread, dims, preferred_element_type=F32)
        wide = wide + lax.dot_general(low, spread, dims, preferred_element_type=F32)
        rate = R_FINE * wide[COND_AT:COND_AT + SLOTS]
        row = jnp.broadcast_to(got[SCAL_AT:SCAL_AT + 1], (SLOTS, NZ))
        at, of = iota((SLOTS, NZ), 1), iota((SLOTS, NZ), 0)

        def scalar(i):
            return jnp.sum(jnp.where(at == of + 8 * i, row, 0.0), axis=1, keepdims=True)

        power, start, depth, named = (scalar(i) for i in range(4))
        source = jnp.where((cell_f >= start) & (cell_f < start + depth), power, 0.0)
        named = jnp.broadcast_to(named, (SLOTS, NZ)) > 0.5
        base_row = peer * (8 * SLOTS)

        def read(ref, ab):
            return jnp.concatenate(
                [ref[pl.ds(base_row + 4 * half + ab, SLOTS, stride=8), :] for half in range(2)], axis=1
            )

        temp = [read(ft, ab) for ab in range(4)]
        strain = [read(fs, ab) for ab in range(4)]
        for step in range(2):
            at = GHOST_AT + 3 * SLOTS * step
            base, along_x, along_y = (wide[at + SLOTS * i:at + SLOTS * (i + 1)] for i in range(3))
            ghosts = (base, base + along_y, base + along_x, base + along_x + along_y)
            after = []
            for ab in range(4):
                mine = temp[ab]
                beside = temp[ab ^ 2] + temp[ab ^ 1] + ghosts[ab]
                beside = beside + jnp.where(cell == 0, 0.0, pltpu.roll(mine, 1, 1))
                beside = beside + jnp.where(cell == 2 * NZ - 1, 0.0, pltpu.roll(mine, 2 * NZ - 1, 1))
                after.append(mine + rate * (beside - 6.0 * mine) + source)
            temp = after
            for ab in range(4):
                stress = (1.0 - temp[ab]) - strain[ab]
                limit = YIELD_BASE * jnp.maximum(1.0 - temp[ab] * (1.0 / MELT_TEMP), YIELD_FLOOR)
                strain[ab] = strain[ab] + (stress - jnp.clip(stress, -limit, limit))
        for ab in range(4):
            for half in range(2):
                rows = pl.ds(base_row + 4 * half + ab, SLOTS, stride=8)
                tout[rows, :] = jnp.where(named, temp[ab][:, half * NZ:(half + 1) * NZ], 0.0)
                sout[rows, :] = jnp.where(named, strain[ab][:, half * NZ:(half + 1) * NZ], 0.0)

    own_rest.wait()
    advance(dev)

    def take_rest(step, carry):
        peer = origin(step)
        message(peer, peer, FIRST, MSG - FIRST, bsend, brecv).wait_recv()
        advance(peer)
        return carry

    lax.fori_loop(1, DEVS, take_rest, 0)

    def sent(step, carry):
        peer = target(step)
        message(peer, dev, 0, FIRST, asend, arecv).wait_send()
        message(peer, dev, FIRST, MSG - FIRST, bsend, brecv).wait_send()
        return carry

    lax.fori_loop(1, DEVS, sent, 0)
    for copy in halos:
        copy.wait_send()


def to_tiles(fine):
    return fine.reshape(COLS, 4, 2, NZ).transpose(0, 2, 1, 3).reshape(COLS * 8, NZ)


def from_tiles(tiles, shape):
    return tiles.reshape(COLS, 2, 4, NZ).transpose(0, 2, 1, 3).reshape(shape)


def local(coarse_temp, coarse_cond, routes, track_start, track_depth, power, fine_temp, fine_strain):
    par = jnp.stack(
        [v.reshape(ROWS).astype(F32) for v in (power, track_start, track_depth, routes)]
        + [jnp.zeros((ROWS,), F32)] * 4
    )
    vmem = pl.BlockSpec(memory_space=pltpu.VMEM)
    dma = pltpu.SemaphoreType.DMA
    cnew, tout, sout = pl.pallas_call(
        kernel,
        out_shape=(
            jax.ShapeDtypeStruct((BX, BY, NZ), F32),
            jax.ShapeDtypeStruct((COLS * 8, NZ), F32),
            jax.ShapeDtypeStruct((COLS * 8, NZ), F32),
        ),
        in_specs=[vmem] * 5,
        out_specs=(vmem,) * 3,
        scratch_shapes=[
            pltpu.VMEM((DEVS * MSG, NZ), F32),
            pltpu.VMEM((DEVS, MSG, NZ), F32),
            pltpu.VMEM((2, 24, NZ), F32),
            pltpu.VMEM((2, 24, NZ), F32),
            pltpu.VMEM((2, 48, NZ), F32),
            pltpu.VMEM((2, 48, NZ), F32),
            pltpu.VMEM((4, 8, NZ), F32),
            pltpu.VMEM((4, 8, NZ), F32),
            pltpu.VMEM((BX + 4, 32, NZ), F32),
            pltpu.VMEM((BX + 2, 32, NZ), F32),
            pltpu.VMEM((BX + 2, 32, NZ), F32),
            pltpu.VMEM((ROWS, 6 * NZ), F32),
            pltpu.VMEM((2, ROWS, NZ), F32),
            dma((8,)),
            dma((8,)),
            dma((DEVS,)),
            dma((DEVS,)),
            dma((DEVS,)),
            dma((DEVS,)),
            dma,
        ],
        compiler_params=pltpu.CompilerParams(
            collective_id=1, has_side_effects=True, vmem_limit_bytes=40 * 2**20
        ),
        name="amr_step",
    )(par, coarse_temp, coarse_cond, to_tiles(fine_temp), to_tiles(fine_strain))
    return cnew, from_tiles(tout, fine_temp.shape), from_tiles(sout, fine_strain.shape)


def solution(mesh):
    placed = (
        P("group", "dev", None),
        P("group", "dev", None),
        P("group", "dev", None, None, None),
        P("group", "dev", None, None),
        P("group", "dev", None, None),
        P("group", "dev", None, None),
        P("group", "dev", None, None, None, None),
        P("group", "dev", None, None, None, None),
    )
    return jax.shard_map(
        local,
        mesh=mesh,
        in_specs=placed,
        out_specs=(
            P("group", "dev", None),
            P("group", "dev", None, None, None, None),
            P("group", "dev", None, None, None, None),
        ),
        check_vma=False,
    )
```

```python
import functools

import jax
import jax.numpy as jnp
from jax import lax
from jax.experimental import pallas as pl
from jax.experimental.pallas import tpu as pltpu
from jax.sharding import PartitionSpec as P

R_COARSE = 0.08
R_FINE = 0.16
YIELD_BASE = 0.6
MELT_TEMP = 3.0
YIELD_FLOOR = 0.05

MESH = pl.DeviceIdType.MESH
VMEM_BYTES = 40 * 2**20
F32 = jnp.float32
BF16 = jnp.bfloat16

X_CHIPS, Z_CHIPS = 4, 8
DEVS = X_CHIPS * Z_CHIPS
SLOTS = 6
COLS = DEVS * SLOTS
BX, BY, NZ = 8, 16, 128
ROWS = BX * BY

MEAN_AT = 0
COND_AT = 12
SCAL_AT = 18
GHOST_AT = 20
FIRST = 16
MSG = 56

CORNERS = ((1, 1), (1, -1), (-1, 1), (-1, -1))


def offset_of(step):
    away = (step + X_CHIPS) // (2 * X_CHIPS)
    turn = (step + X_CHIPS) % (2 * X_CHIPS)
    middle = (away == 0) | (away == Z_CHIPS // 2)
    ox = jnp.where(middle, step % X_CHIPS, turn // 2)
    return ox, jnp.where(middle, away, away * (1 - 2 * (turn % 2)))


def turn_of(z):
    return jnp.where(z < 6, z, 13 - z)


def split(value):
    high = value.astype(BF16)
    return high, (value - high.astype(F32)).astype(BF16)


def pick(chooser, value, dims=((1,), (0,))):
    total = None
    for part in split(value):
        term = lax.dot_general(chooser, part, (dims, ((), ())), preferred_element_type=F32)
        total = term if total is None else total + term
    return total


def iota(shape, dim):
    return lax.broadcasted_iota(jnp.int32, shape, dim)


def kernel(
    power_in, start_in, depth_in, routes_in, ct_in, cc_in, ft_in, fs_in, cnew, tout, sout,
        power_v, start_v, depth_v, routes_v, ct, cc, ft, fs, outb, land, hys, hyl, hxs, hxl, hcs, hcl, oe, ce, me, field, side,
    hsend, hrecv, asend, arecv, bsend, brecv, lsem, isem,
):
    group = lax.axis_index("group")
    groups = lax.axis_size("group")
    dev = lax.axis_index("dev")
    dx, dz = dev // Z_CHIPS, dev % Z_CHIPS

    def target(step):
        ox, oz = offset_of(step)
        return ((dx + ox) % X_CHIPS) * Z_CHIPS + (dz + oz + Z_CHIPS) % Z_CHIPS

    def origin(step):
        ox, oz = offset_of(step)
        return ((dx - ox + X_CHIPS) % X_CHIPS) * Z_CHIPS + (dz - oz + Z_CHIPS) % Z_CHIPS

    def near(dg, dd):
        return {"group": (group + dg + groups) % groups, "dev": (dev + dd + DEVS) % DEVS}

    barrier = pltpu.get_barrier_semaphore()

    def greet(step, carry):
        pl.semaphore_signal(barrier, inc=1, device_id={"dev": target(step)}, device_id_type=MESH)
        return carry

    lax.fori_loop(1, DEVS, greet, 0)
    for dg, dd in ((1, 0), (-1, 0)) + CORNERS:
        pl.semaphore_signal(barrier, inc=1, device_id=near(dg, dd), device_id_type=MESH)

    loads = []
    arrays = ((routes_in, routes_v), (power_in, power_v), (start_in, start_v), (depth_in, depth_v))
    arrays = arrays + ((ct_in, ct), (cc_in, cc), (ft_in, ft), (fs_in, fs))
    for i, (src, dst) in enumerate(arrays):
        load = pltpu.make_async_copy(src, dst, isem.at[i])
        load.start()
        loads.append(load)
    for load in loads[:6]:
        load.wait()

    for x in range(BX):
        hys[0, 2 * x:2 * x + 2] = ct[x, BY - 2:BY]
        hys[0, 16 + x:17 + x] = cc[x, BY - 1:BY]
        hys[1, 2 * x:2 * x + 2] = ct[x, 0:2]
        hys[1, 16 + x:17 + x] = cc[x, 0:1]
    for i, (lo, edge) in enumerate(((BX - 2, BX - 1), (0, 0))):
        hxs[i, 0:16] = ct[lo]
        hxs[i, 16:32] = ct[lo + 1]
        hxs[i, 32:48] = cc[edge]
    for i, (dg, dd) in enumerate(CORNERS):
        row = BX - 1 if dg > 0 else 0
        hcs[i] = jnp.broadcast_to(ct[row, BY - 1:BY] if dd > 0 else ct[row, 0:1], (8, NZ))

    held = [power_v[...], start_v[...].astype(F32), depth_v[...].astype(F32), routes_v[:, 0, :].astype(F32)]
    same_y = jnp.where(iota((BY, ROWS), 1) % BY == iota((BY, ROWS), 0), 1.0, 0.0).astype(BF16)
    dims = (((1,), (0,)), ((), ()))
    flat = None
    for part in split(jnp.concatenate(held, axis=0)):
        term = lax.dot_general(part, same_y, dims, preferred_element_type=F32)
        flat = term if flat is None else flat + term
    same_x = iota((4 * BX, ROWS), 1) // BY == iota((4 * BX, ROWS), 0) % BX
    flat = jnp.where(same_x, flat, 0.0)
    power, start, depth, owner = (jnp.sum(flat[BX * i:BX * (i + 1)], axis=0, keepdims=True) for i in range(4))
    owner_b = jnp.broadcast_to(owner, (DEVS, ROWS))
    hot = jnp.where(owner_b == iota((DEVS, ROWS), 0).astype(F32), 1.0, 0.0)
    earlier = jnp.where(iota((ROWS, ROWS), 0) < iota((ROWS, ROWS), 1), 1.0, 0.0).astype(BF16)
    before = lax.dot_general(hot.astype(BF16), earlier, (((1,), (0,)), ((), ())), preferred_element_type=F32)
    slot = jnp.sum(before * hot, axis=0, keepdims=True)
    code = slot * DEVS + owner
    to_slot = jnp.where(jnp.broadcast_to(code, (COLS, ROWS)) == iota((COLS, ROWS), 0).astype(F32), 1.0, 0.0).astype(BF16)
    code_t = jnp.transpose(jnp.broadcast_to(code, (ROWS, ROWS)))
    start_t = jnp.transpose(jnp.broadcast_to(start, (ROWS, ROWS)))
    depth_t = jnp.transpose(jnp.broadcast_to(depth, (ROWS, ROWS)))
    power_t = jnp.transpose(jnp.broadcast_to(power, (ROWS, ROWS)))
    lanes = iota((ROWS, ROWS), 1).astype(F32)
    from_slot = jnp.concatenate(
        [jnp.where(code_t == lanes, 1.0, 0.0), jnp.where(code_t == lanes + ROWS, 1.0, 0.0)], axis=1
    ).astype(BF16)

    conds = pick(to_slot, cc[...].reshape(ROWS, NZ))
    for k in range(SLOTS):
        outb[pl.ds(COND_AT + k, DEVS, stride=MSG), :] = conds[k * DEVS:(k + 1) * DEVS]
    at_slot = jnp.broadcast_to(slot, (8, ROWS)) == iota((8, ROWS), 0).astype(F32)
    blocks = [jnp.where(at_slot, jnp.broadcast_to(v, (8, ROWS)), 0.0) for v in (power, start, depth)]
    blocks = blocks + [jnp.where(at_slot, 1.0, 0.0), jnp.zeros((NZ - 32, ROWS), F32)]
    scalars = pick(hot.astype(BF16), jnp.concatenate(blocks, axis=0), ((1,), (1,)))
    outb[pl.ds(SCAL_AT, DEVS, stride=MSG), :] = scalars
    outb[pl.ds(SCAL_AT + 1, DEVS, stride=MSG), :] = jnp.zeros_like(scalars)

    loads[6].wait()
    for k in range(SLOTS):
        for half in range(2):
            total = None
            for ab in range(4):
                term = ft[pl.ds(8 * k + 4 * half + ab, DEVS, stride=8 * SLOTS), :]
                total = term if total is None else total + term
            outb[pl.ds(MEAN_AT + SLOTS * half + k, DEVS, stride=MSG), :] = 0.25 * total

    oe[...] = jnp.zeros_like(oe)
    ce[...] = jnp.zeros_like(ce)
    for x in range(BX):
        oe[2 + x, 8:24] = ct[x]
        ce[1 + x, 8:24] = cc[x]

    def own(lo, n):
        src = outb.at[pl.ds(pl.multiple_of(dev * MSG + lo, 8), n)]
        return pltpu.make_async_copy(src, land.at[dev, pl.ds(lo, n)], lsem)

    def message(peer, sender, lo, n, send, recv):
        src = outb.at[pl.ds(pl.multiple_of(peer * MSG + lo, 8), n)]
        return pltpu.make_async_remote_copy(
            src, land.at[sender, pl.ds(lo, n)], send.at[peer], recv.at[sender],
            device_id={"dev": peer}, device_id_type=MESH,
        )

    pl.semaphore_wait(barrier, DEVS - 1 + 2 + len(CORNERS))

    halos = []
    plan = [(hys, hyl, 0, 0, 1), (hys, hyl, 1, 0, -1), (hxs, hxl, 0, 1, 0), (hxs, hxl, 1, -1, 0)]
    plan = plan + [(hcs, hcl, i, dg, dd) for i, (dg, dd) in enumerate(CORNERS)]
    for number, (src, dst, i, dg, dd) in enumerate(plan):
        copy = pltpu.make_async_remote_copy(
            src.at[i], dst.at[i], hsend.at[number], hrecv.at[number],
            device_id=near(dg, dd), device_id_type=MESH,
        )
        copy.start()
        halos.append(copy)

    def send_first(step, carry):
        message(target(step), dev, 0, FIRST, asend, arecv).start()
        return carry

    lax.fori_loop(1, DEVS, send_first, 0)
    own_first = own(0, FIRST)
    own_first.start()

    for copy in halos:
        copy.wait_recv()

    low_x, high_x = group > 0, group < groups - 1
    low_y, high_y = dev > 0, dev < DEVS - 1

    def inside(ok, value):
        return jnp.where(ok, value, 0.0)

    for x in range(BX):
        oe[2 + x, 6:8] = inside(low_y, hyl[0, 2 * x:2 * x + 2])
        oe[2 + x, 24:26] = inside(high_y, hyl[1, 2 * x:2 * x + 2])
        ce[1 + x, 7:8] = inside(low_y, hyl[0, 16 + x:17 + x])
        ce[1 + x, 24:25] = inside(high_y, hyl[1, 16 + x:17 + x])
    oe[0, 8:24] = inside(low_x, hxl[0, 0:16])
    oe[1, 8:24] = inside(low_x, hxl[0, 16:32])
    ce[0, 8:24] = inside(low_x, hxl[0, 32:48])
    oe[BX + 2, 8:24] = inside(high_x, hxl[1, 0:16])
    oe[BX + 3, 8:24] = inside(high_x, hxl[1, 16:32])
    ce[BX + 1, 8:24] = inside(high_x, hxl[1, 32:48])
    oe[1, 7:8] = inside(low_x & low_y, hcl[0, 0:1])
    oe[1, 24:25] = inside(low_x & high_y, hcl[1, 0:1])
    oe[BX + 2, 7:8] = inside(high_x & low_y, hcl[2, 0:1])
    oe[BX + 2, 24:25] = inside(high_x & high_y, hcl[3, 0:1])

    lane = iota((32, NZ), 1)
    for x in range(BX + 2):
        cur = oe[x + 1]
        beside = oe[x] + oe[x + 2] + pltpu.roll(cur, 1, 0) + pltpu.roll(cur, 31, 0)
        beside = beside + jnp.where(lane == 0, 0.0, pltpu.roll(cur, 1, 1))
        beside = beside + jnp.where(lane == NZ - 1, 0.0, pltpu.roll(cur, NZ - 1, 1))
        new = cur + R_COARSE * ce[x] * (beside - 6.0 * cur)
        me[x] = 0.5 * (cur + new)

    for x in range(BX):
        for step, (arr, at) in enumerate(((oe, x + 2), (me, x + 1))):
            west, east = arr[at - 1, 8:24], arr[at + 1, 8:24]
            south, north = arr[at, 7:23], arr[at, 9:25]
            base, along_x, along_y = west + south, east - west, north - south
            for i, value in enumerate((base, along_x, along_y)):
                f = 3 * step + i
                field[x * BY:(x + 1) * BY, f * NZ:(f + 1) * NZ] = value
            side[step, x * BY:(x + 1) * BY] = base + 0.5 * (along_x + along_y)

    ghosts = pick(to_slot, field[...])
    for f in range(6):
        for k in range(SLOTS):
            outb[pl.ds(GHOST_AT + SLOTS * f + k, DEVS, stride=MSG), :] = ghosts[k * DEVS:(k + 1) * DEVS, f * NZ:(f + 1) * NZ]

    def send_rest(step, carry):
        message(target(step), dev, FIRST, MSG - FIRST, bsend, brecv).start()
        return carry

    def by_turn(i, carry):
        peer = (dx + i) % X_CHIPS * Z_CHIPS + turn_of(i // X_CHIPS)

        @pl.when(peer != dev)
        def _():
            message(peer, dev, FIRST, MSG - FIRST, bsend, brecv).start()

        return carry

    lax.fori_loop(0, DEVS, by_turn, 0)
    own_first.wait()
    own_rest = own(FIRST, MSG - FIRST)
    own_rest.start()

    def take_first(step, carry):
        message(origin(step), origin(step), 0, FIRST, asend, arecv).wait_recv()
        return carry

    lax.fori_loop(1, DEVS, take_first, 0)
    halves = []
    for half in range(2):
        rows = [land[:, MEAN_AT + SLOTS * half + k, :] for k in range(SLOTS)] + [jnp.zeros((2 * ROWS - COLS, NZ), F32)]
        halves.append(jnp.concatenate(rows, axis=0))
    fine = pick(from_slot, jnp.concatenate(halves, axis=1))
    row_i, col_i = iota((2 * NZ, 2 * NZ), 0), iota((2 * NZ, 2 * NZ), 1)
    wanted = jnp.where(col_i < NZ, 2 * col_i, 2 * (col_i - NZ) + 1)
    high, low = split(fine)
    apart = jnp.where(row_i == wanted, 1.0, 0.0).astype(BF16)
    dims = (((1,), (0,)), ((), ()))
    both = lax.dot_general(high, apart, dims, preferred_element_type=F32)
    both = both + lax.dot_general(low, apart, dims, preferred_element_type=F32)
    even, odd = both[:, :NZ], both[:, NZ:]
    rate = R_FINE * cc[...].reshape(ROWS, NZ)
    place = iota((ROWS, NZ), 1)

    def heat(fine_cell):
        cell = fine_cell.astype(F32)
        return jnp.where((cell >= start_t) & (cell < start_t + depth_t), power_t, 0.0)

    heat_even, heat_odd = heat(2 * place), heat(2 * place + 1)
    for step in range(2):
        under = jnp.where(place == 0, 0.0, pltpu.roll(odd, 1, 1))
        over = jnp.where(place == NZ - 1, 0.0, pltpu.roll(even, NZ - 1, 1))
        ghost = side[step]
        even, odd = (
            even + rate * (ghost + odd + under - 4.0 * even) + heat_even,
            odd + rate * (ghost + even + over - 4.0 * odd) + heat_odd,
        )
    cnew[...] = (0.5 * (even + odd)).reshape(BX, BY, NZ)

    spread = jnp.where(iota((NZ, 2 * NZ), 1) // 2 == iota((NZ, 2 * NZ), 0), 1.0, 0.0).astype(BF16)
    cell = iota((SLOTS, 2 * NZ), 1)
    cell_f = cell.astype(F32)
    dims = (((1,), (0,)), ((), ()))

    def advance(peer):
        got = land[peer]
        high, low = split(got)
        wide = lax.dot_general(high, spread, dims, preferred_element_type=F32)
        wide = wide + lax.dot_general(low, spread, dims, preferred_element_type=F32)
        rate = R_FINE * wide[COND_AT:COND_AT + SLOTS]
        row = jnp.broadcast_to(got[SCAL_AT:SCAL_AT + 1], (SLOTS, NZ))
        at, of = iota((SLOTS, NZ), 1), iota((SLOTS, NZ), 0)

        def scalar(i):
            return jnp.sum(jnp.where(at == of + 8 * i, row, 0.0), axis=1, keepdims=True)

        power, start, depth, named = (scalar(i) for i in range(4))
        source = jnp.where((cell_f >= start) & (cell_f < start + depth), power, 0.0)
        named = jnp.broadcast_to(named, (SLOTS, NZ)) > 0.5
        base_row = peer * (8 * SLOTS)

        def read(ref, ab):
            return jnp.concatenate(
                [ref[pl.ds(base_row + 4 * half + ab, SLOTS, stride=8), :] for half in range(2)], axis=1
            )

        temp = [read(ft, ab) for ab in range(4)]
        strain = [read(fs, ab) for ab in range(4)]
        for step in range(2):
            at = GHOST_AT + 3 * SLOTS * step
            base, along_x, along_y = (wide[at + SLOTS * i:at + SLOTS * (i + 1)] for i in range(3))
            ghosts = (base, base + along_y, base + along_x, base + along_x + along_y)
            after = []
            for ab in range(4):
                mine = temp[ab]
                beside = temp[ab ^ 2] + temp[ab ^ 1] + ghosts[ab]
                beside = beside + jnp.where(cell == 0, 0.0, pltpu.roll(mine, 1, 1))
                beside = beside + jnp.where(cell == 2 * NZ - 1, 0.0, pltpu.roll(mine, 2 * NZ - 1, 1))
                after.append(mine + rate * (beside - 6.0 * mine) + source)
            temp = after
            for ab in range(4):
                stress = (1.0 - temp[ab]) - strain[ab]
                limit = YIELD_BASE * jnp.maximum(1.0 - temp[ab] * (1.0 / MELT_TEMP), YIELD_FLOOR)
                strain[ab] = strain[ab] + (stress - jnp.clip(stress, -limit, limit))
        for ab in range(4):
            for half in range(2):
                rows = pl.ds(base_row + 4 * half + ab, SLOTS, stride=8)
                tout[rows, :] = jnp.where(named, temp[ab][:, half * NZ:(half + 1) * NZ], 0.0)
                sout[rows, :] = jnp.where(named, strain[ab][:, half * NZ:(half + 1) * NZ], 0.0)

    own_rest.wait()
    loads[7].wait()

    def take_rest(turn, carry):
        for i in range(X_CHIPS):
            step = turn * X_CHIPS + i

            @pl.when(step > 0)
            def _():
                peer = origin(step)
                message(peer, peer, FIRST, MSG - FIRST, bsend, brecv).wait_recv()

        for i in range(X_CHIPS):
            advance(origin(turn * X_CHIPS + i))
        return carry

    lax.fori_loop(0, Z_CHIPS, take_rest, 0)

    def sent(step, carry):
        peer = target(step)
        message(peer, dev, 0, FIRST, asend, arecv).wait_send()
        message(peer, dev, FIRST, MSG - FIRST, bsend, brecv).wait_send()
        return carry

    lax.fori_loop(1, DEVS, sent, 0)
    for copy in halos:
        copy.wait_send()


def to_tiles(fine):
    return fine.reshape(COLS, 4, 2, NZ).transpose(0, 2, 1, 3).reshape(COLS * 8, NZ)


def from_tiles(tiles, shape):
    return tiles.reshape(COLS, 2, 4, NZ).transpose(0, 2, 1, 3).reshape(shape)


def finish(cin, tin, sin, cout, tout, sout, sem):
    copies = [
        pltpu.make_async_copy(src, dst, sem.at[i])
        for i, (src, dst) in enumerate(((tin, tout), (sin, sout), (cin, cout)))
    ]
    for copy in copies:
        copy.start()
    for copy in copies:
        copy.wait()


def local(coarse_temp, coarse_cond, routes, track_start, track_depth, power, fine_temp, fine_strain):
    hbm = pl.BlockSpec(memory_space=pltpu.HBM)
    dma = pltpu.SemaphoreType.DMA
    shapes = ((BX, BY, NZ), (COLS * 8, NZ), (COLS * 8, NZ))
    vmem = pl.BlockSpec(memory_space=pltpu.VMEM)
    held = pl.pallas_call(
        kernel,
        out_shape=tuple(pltpu.VMEM(shape, F32) for shape in shapes),
        in_specs=[hbm] * 8,
        out_specs=(vmem,) * 3,
        scratch_shapes=[
            pltpu.VMEM((BX, BY), F32),
            pltpu.VMEM((BX, BY), jnp.int32),
            pltpu.VMEM((BX, BY), jnp.int32),
            pltpu.VMEM((BX, 1, BY), jnp.int32),
            pltpu.VMEM((BX, BY, NZ), F32),
            pltpu.VMEM((BX, BY, NZ), F32),
            pltpu.VMEM((COLS * 8, NZ), F32),
            pltpu.VMEM((COLS * 8, NZ), F32),
            pltpu.VMEM((DEVS * MSG, NZ), F32),
            pltpu.VMEM((DEVS, MSG, NZ), F32),
            pltpu.VMEM((2, 24, NZ), F32),
            pltpu.VMEM((2, 24, NZ), F32),
            pltpu.VMEM((2, 48, NZ), F32),
            pltpu.VMEM((2, 48, NZ), F32),
            pltpu.VMEM((4, 8, NZ), F32),
            pltpu.VMEM((4, 8, NZ), F32),
            pltpu.VMEM((BX + 4, 32, NZ), F32),
            pltpu.VMEM((BX + 2, 32, NZ), F32),
            pltpu.VMEM((BX + 2, 32, NZ), F32),
            pltpu.VMEM((ROWS, 6 * NZ), F32),
            pltpu.VMEM((2, ROWS, NZ), F32),
            dma((8,)),
            dma((8,)),
            dma((DEVS,)),
            dma((DEVS,)),
            dma((DEVS,)),
            dma((DEVS,)),
            dma,
            dma((8,)),
        ],
        compiler_params=pltpu.CompilerParams(
            collective_id=1, has_side_effects=True, vmem_limit_bytes=VMEM_BYTES
        ),
        name="amr_step",
    )(
        *(
            pltpu.with_memory_space_constraint(value, pltpu.HBM)
            for value in (
                power.reshape(BX, BY),
                track_start.reshape(BX, BY),
                track_depth.reshape(BX, BY),
                routes.reshape(BX, 1, BY),
                coarse_temp,
                coarse_cond,
                to_tiles(fine_temp),
                to_tiles(fine_strain),
            )
        )
    )
    cnew, tout, sout = pl.pallas_call(
        finish,
        out_shape=tuple(pltpu.HBM(shape, F32) for shape in shapes),
        in_specs=[vmem] * 3,
        out_specs=(hbm,) * 3,
        scratch_shapes=[dma((3,))],
        name="write_results",
    )(*(pltpu.with_memory_space_constraint(value, pltpu.VMEM) for value in held))
    return cnew, from_tiles(tout, fine_temp.shape), from_tiles(sout, fine_strain.shape)


def solution(mesh):
    placed = (
        P("group", "dev", None),
        P("group", "dev", None),
        P("group", "dev", None, None, None),
        P("group", "dev", None, None),
        P("group", "dev", None, None),
        P("group", "dev", None, None),
        P("group", "dev", None, None, None, None),
        P("group", "dev", None, None, None, None),
    )
    return jax.shard_map(
        local,
        mesh=mesh,
        in_specs=placed,
        out_specs=(
            P("group", "dev", None),
            P("group", "dev", None, None, None, None),
            P("group", "dev", None, None, None, None),
        ),
        check_vma=False,
    )
```

```python
import functools

import jax
import jax.numpy as jnp
from jax import lax
from jax.experimental import pallas as pl
from jax.experimental.pallas import tpu as pltpu
from jax.sharding import PartitionSpec as P

R_COARSE = 0.08
R_FINE = 0.16
YIELD_BASE = 0.6
MELT_TEMP = 3.0
YIELD_FLOOR = 0.05

MESH = pl.DeviceIdType.MESH
VMEM_BYTES = 40 * 2**20
F32 = jnp.float32
BF16 = jnp.bfloat16

X_CHIPS, Z_CHIPS = 4, 8
DEVS = X_CHIPS * Z_CHIPS
SLOTS = 6
COLS = DEVS * SLOTS
BX, BY, NZ = 8, 16, 128
ROWS = BX * BY

MEAN_AT = 0
COND_AT = 12
SCAL_AT = 18
GHOST_AT = 20
FIRST = 16
MSG = 56

CORNERS = ((1, 1), (1, -1), (-1, 1), (-1, -1))


def offset_of(step):
    away = (step + X_CHIPS) // (2 * X_CHIPS)
    turn = (step + X_CHIPS) % (2 * X_CHIPS)
    middle = (away == 0) | (away == Z_CHIPS // 2)
    ox = jnp.where(middle, step % X_CHIPS, turn // 2)
    return ox, jnp.where(middle, away, away * (1 - 2 * (turn % 2)))


def turn_of(z):
    return jnp.where(z < 6, z, 13 - z)


def split(value):
    high = value.astype(BF16)
    return high, (value - high.astype(F32)).astype(BF16)


def pick(chooser, value, dims=((1,), (0,))):
    total = None
    for part in split(value):
        term = lax.dot_general(chooser, part, (dims, ((), ())), preferred_element_type=F32)
        total = term if total is None else total + term
    return total


def iota(shape, dim):
    return lax.broadcasted_iota(jnp.int32, shape, dim)


def kernel(
    power_in, start_in, depth_in, routes_in, ct_in, cc_in, ft_in, fs_in, cnew, tout, sout,
        power_v, start_v, depth_v, routes_v, ct, cc, ft, fs, outb, land, hys, hyl, hxs, hxl, hcs, hcl, oe, ce, me, field, side,
    hsend, hrecv, asend, arecv, bsend, brecv, lsem, isem,
):
    group = lax.axis_index("group")
    groups = lax.axis_size("group")
    dev = lax.axis_index("dev")
    dx, dz = dev // Z_CHIPS, dev % Z_CHIPS

    def target(step):
        ox, oz = offset_of(step)
        return ((dx + ox) % X_CHIPS) * Z_CHIPS + (dz + oz + Z_CHIPS) % Z_CHIPS

    def origin(step):
        ox, oz = offset_of(step)
        return ((dx - ox + X_CHIPS) % X_CHIPS) * Z_CHIPS + (dz - oz + Z_CHIPS) % Z_CHIPS

    def near(dg, dd):
        return {"group": (group + dg + groups) % groups, "dev": (dev + dd + DEVS) % DEVS}

    barrier = pltpu.get_barrier_semaphore()

    def greet(step, carry):
        pl.semaphore_signal(barrier, inc=1, device_id={"dev": target(step)}, device_id_type=MESH)
        return carry

    lax.fori_loop(1, DEVS, greet, 0)
    for dg, dd in ((1, 0), (-1, 0)) + CORNERS:
        pl.semaphore_signal(barrier, inc=1, device_id=near(dg, dd), device_id_type=MESH)

    loads = []
    arrays = ((routes_in, routes_v), (power_in, power_v), (start_in, start_v), (depth_in, depth_v))
    arrays = arrays + ((ct_in, ct), (cc_in, cc), (ft_in, ft), (fs_in, fs))
    for i, (src, dst) in enumerate(arrays):
        load = pltpu.make_async_copy(src, dst, isem.at[i])
        load.start()
        loads.append(load)
    for load in loads[:6]:
        load.wait()

    for x in range(BX):
        hys[0, 2 * x:2 * x + 2] = ct[x, BY - 2:BY]
        hys[0, 16 + x:17 + x] = cc[x, BY - 1:BY]
        hys[1, 2 * x:2 * x + 2] = ct[x, 0:2]
        hys[1, 16 + x:17 + x] = cc[x, 0:1]
    for i, (lo, edge) in enumerate(((BX - 2, BX - 1), (0, 0))):
        hxs[i, 0:16] = ct[lo]
        hxs[i, 16:32] = ct[lo + 1]
        hxs[i, 32:48] = cc[edge]
    for i, (dg, dd) in enumerate(CORNERS):
        row = BX - 1 if dg > 0 else 0
        hcs[i] = jnp.broadcast_to(ct[row, BY - 1:BY] if dd > 0 else ct[row, 0:1], (8, NZ))

    held = [power_v[...], start_v[...].astype(F32), depth_v[...].astype(F32), routes_v[:, 0, :].astype(F32)]
    same_y = jnp.where(iota((BY, ROWS), 1) % BY == iota((BY, ROWS), 0), 1.0, 0.0).astype(BF16)
    dims = (((1,), (0,)), ((), ()))
    flat = None
    for part in split(jnp.concatenate(held, axis=0)):
        term = lax.dot_general(part, same_y, dims, preferred_element_type=F32)
        flat = term if flat is None else flat + term
    same_x = iota((4 * BX, ROWS), 1) // BY == iota((4 * BX, ROWS), 0) % BX
    flat = jnp.where(same_x, flat, 0.0)
    power, start, depth, owner = (jnp.sum(flat[BX * i:BX * (i + 1)], axis=0, keepdims=True) for i in range(4))
    owner_b = jnp.broadcast_to(owner, (DEVS, ROWS))
    hot = jnp.where(owner_b == iota((DEVS, ROWS), 0).astype(F32), 1.0, 0.0)
    earlier = jnp.where(iota((ROWS, ROWS), 0) < iota((ROWS, ROWS), 1), 1.0, 0.0).astype(BF16)
    before = lax.dot_general(hot.astype(BF16), earlier, (((1,), (0,)), ((), ())), preferred_element_type=F32)
    slot = jnp.sum(before * hot, axis=0, keepdims=True)
    code = slot * DEVS + owner
    to_slot = jnp.where(jnp.broadcast_to(code, (COLS, ROWS)) == iota((COLS, ROWS), 0).astype(F32), 1.0, 0.0).astype(BF16)
    code_t = jnp.transpose(jnp.broadcast_to(code, (ROWS, ROWS)))
    start_t = jnp.transpose(jnp.broadcast_to(start, (ROWS, ROWS)))
    depth_t = jnp.transpose(jnp.broadcast_to(depth, (ROWS, ROWS)))
    power_t = jnp.transpose(jnp.broadcast_to(power, (ROWS, ROWS)))
    lanes = iota((ROWS, ROWS), 1).astype(F32)
    from_slot = jnp.concatenate(
        [jnp.where(code_t == lanes, 1.0, 0.0), jnp.where(code_t == lanes + ROWS, 1.0, 0.0)], axis=1
    ).astype(BF16)

    conds = pick(to_slot, cc[...].reshape(ROWS, NZ))
    for k in range(SLOTS):
        outb[pl.ds(COND_AT + k, DEVS, stride=MSG), :] = conds[k * DEVS:(k + 1) * DEVS]
    at_slot = jnp.broadcast_to(slot, (8, ROWS)) == iota((8, ROWS), 0).astype(F32)
    blocks = [jnp.where(at_slot, jnp.broadcast_to(v, (8, ROWS)), 0.0) for v in (power, start, depth)]
    blocks = blocks + [jnp.where(at_slot, 1.0, 0.0), jnp.zeros((NZ - 32, ROWS), F32)]
    scalars = pick(hot.astype(BF16), jnp.concatenate(blocks, axis=0), ((1,), (1,)))
    outb[pl.ds(SCAL_AT, DEVS, stride=MSG), :] = scalars
    outb[pl.ds(SCAL_AT + 1, DEVS, stride=MSG), :] = jnp.zeros_like(scalars)

    loads[6].wait()
    for k in range(SLOTS):
        for half in range(2):
            total = None
            for ab in range(4):
                term = ft[pl.ds(8 * k + 4 * half + ab, DEVS, stride=8 * SLOTS), :]
                total = term if total is None else total + term
            outb[pl.ds(MEAN_AT + SLOTS * half + k, DEVS, stride=MSG), :] = 0.25 * total

    oe[...] = jnp.zeros_like(oe)
    ce[...] = jnp.zeros_like(ce)
    for x in range(BX):
        oe[2 + x, 8:24] = ct[x]
        ce[1 + x, 8:24] = cc[x]

    def own(lo, n):
        src = outb.at[pl.ds(pl.multiple_of(dev * MSG + lo, 8), n)]
        return pltpu.make_async_copy(src, land.at[dev, pl.ds(lo, n)], lsem)

    def message(peer, sender, lo, n, send, recv):
        src = outb.at[pl.ds(pl.multiple_of(peer * MSG + lo, 8), n)]
        return pltpu.make_async_remote_copy(
            src, land.at[sender, pl.ds(lo, n)], send.at[peer], recv.at[sender],
            device_id={"dev": peer}, device_id_type=MESH,
        )

    pl.semaphore_wait(barrier, DEVS - 1 + 2 + len(CORNERS))

    halos = []
    plan = [(hys, hyl, 0, 0, 1), (hys, hyl, 1, 0, -1), (hxs, hxl, 0, 1, 0), (hxs, hxl, 1, -1, 0)]
    plan = plan + [(hcs, hcl, i, dg, dd) for i, (dg, dd) in enumerate(CORNERS)]
    for number, (src, dst, i, dg, dd) in enumerate(plan):
        copy = pltpu.make_async_remote_copy(
            src.at[i], dst.at[i], hsend.at[number], hrecv.at[number],
            device_id=near(dg, dd), device_id_type=MESH,
        )
        copy.start()
        halos.append(copy)

    def send_first(step, carry):
        message(target(step), dev, 0, FIRST, asend, arecv).start()
        return carry

    def first_by_turn(i, carry):
        peer = (dx + i) % X_CHIPS * Z_CHIPS + turn_of(i // X_CHIPS)

        @pl.when(peer != dev)
        def _():
            message(peer, dev, 0, FIRST, asend, arecv).start()

        return carry

    lax.fori_loop(0, DEVS, first_by_turn, 0)
    own_first = own(0, FIRST)
    own_first.start()

    for copy in halos:
        copy.wait_recv()

    low_x, high_x = group > 0, group < groups - 1
    low_y, high_y = dev > 0, dev < DEVS - 1

    def inside(ok, value):
        return jnp.where(ok, value, 0.0)

    for x in range(BX):
        oe[2 + x, 6:8] = inside(low_y, hyl[0, 2 * x:2 * x + 2])
        oe[2 + x, 24:26] = inside(high_y, hyl[1, 2 * x:2 * x + 2])
        ce[1 + x, 7:8] = inside(low_y, hyl[0, 16 + x:17 + x])
        ce[1 + x, 24:25] = inside(high_y, hyl[1, 16 + x:17 + x])
    oe[0, 8:24] = inside(low_x, hxl[0, 0:16])
    oe[1, 8:24] = inside(low_x, hxl[0, 16:32])
    ce[0, 8:24] = inside(low_x, hxl[0, 32:48])
    oe[BX + 2, 8:24] = inside(high_x, hxl[1, 0:16])
    oe[BX + 3, 8:24] = inside(high_x, hxl[1, 16:32])
    ce[BX + 1, 8:24] = inside(high_x, hxl[1, 32:48])
    oe[1, 7:8] = inside(low_x & low_y, hcl[0, 0:1])
    oe[1, 24:25] = inside(low_x & high_y, hcl[1, 0:1])
    oe[BX + 2, 7:8] = inside(high_x & low_y, hcl[2, 0:1])
    oe[BX + 2, 24:25] = inside(high_x & high_y, hcl[3, 0:1])

    lane = iota((32, NZ), 1)
    for x in range(BX + 2):
        cur = oe[x + 1]
        beside = oe[x] + oe[x + 2] + pltpu.roll(cur, 1, 0) + pltpu.roll(cur, 31, 0)
        beside = beside + jnp.where(lane == 0, 0.0, pltpu.roll(cur, 1, 1))
        beside = beside + jnp.where(lane == NZ - 1, 0.0, pltpu.roll(cur, NZ - 1, 1))
        new = cur + R_COARSE * ce[x] * (beside - 6.0 * cur)
        me[x] = 0.5 * (cur + new)

    for x in range(BX):
        for step, (arr, at) in enumerate(((oe, x + 2), (me, x + 1))):
            west, east = arr[at - 1, 8:24], arr[at + 1, 8:24]
            south, north = arr[at, 7:23], arr[at, 9:25]
            base, along_x, along_y = west + south, east - west, north - south
            for i, value in enumerate((base, along_x, along_y)):
                f = 3 * step + i
                field[x * BY:(x + 1) * BY, f * NZ:(f + 1) * NZ] = value
            side[step, x * BY:(x + 1) * BY] = base + 0.5 * (along_x + along_y)

    ghosts = pick(to_slot, field[...])
    for f in range(6):
        for k in range(SLOTS):
            outb[pl.ds(GHOST_AT + SLOTS * f + k, DEVS, stride=MSG), :] = ghosts[k * DEVS:(k + 1) * DEVS, f * NZ:(f + 1) * NZ]

    def send_rest(step, carry):
        message(target(step), dev, FIRST, MSG - FIRST, bsend, brecv).start()
        return carry

    def by_turn(i, carry):
        peer = (dx + i) % X_CHIPS * Z_CHIPS + turn_of(i // X_CHIPS)

        @pl.when(peer != dev)
        def _():
            message(peer, dev, FIRST, 24, bsend, brecv).start()
            message(peer, dev, FIRST + 24, 16, bsend, brecv).start()

        return carry

    lax.fori_loop(0, DEVS, by_turn, 0)
    own_first.wait()
    own_rest = own(FIRST, MSG - FIRST)
    own_rest.start()

    def take_first(step, carry):
        message(origin(step), origin(step), 0, FIRST, asend, arecv).wait_recv()
        return carry

    lax.fori_loop(1, DEVS, take_first, 0)
    halves = []
    for half in range(2):
        rows = [land[:, MEAN_AT + SLOTS * half + k, :] for k in range(SLOTS)] + [jnp.zeros((2 * ROWS - COLS, NZ), F32)]
        halves.append(jnp.concatenate(rows, axis=0))
    fine = pick(from_slot, jnp.concatenate(halves, axis=1))
    row_i, col_i = iota((2 * NZ, 2 * NZ), 0), iota((2 * NZ, 2 * NZ), 1)
    wanted = jnp.where(col_i < NZ, 2 * col_i, 2 * (col_i - NZ) + 1)
    high, low = split(fine)
    apart = jnp.where(row_i == wanted, 1.0, 0.0).astype(BF16)
    dims = (((1,), (0,)), ((), ()))
    both = lax.dot_general(high, apart, dims, preferred_element_type=F32)
    both = both + lax.dot_general(low, apart, dims, preferred_element_type=F32)
    even, odd = both[:, :NZ], both[:, NZ:]
    rate = R_FINE * cc[...].reshape(ROWS, NZ)
    place = iota((ROWS, NZ), 1)

    def heat(fine_cell):
        cell = fine_cell.astype(F32)
        return jnp.where((cell >= start_t) & (cell < start_t + depth_t), power_t, 0.0)

    heat_even, heat_odd = heat(2 * place), heat(2 * place + 1)
    for step in range(2):
        under = jnp.where(place == 0, 0.0, pltpu.roll(odd, 1, 1))
        over = jnp.where(place == NZ - 1, 0.0, pltpu.roll(even, NZ - 1, 1))
        ghost = side[step]
        even, odd = (
            even + rate * (ghost + odd + under - 4.0 * even) + heat_even,
            odd + rate * (ghost + even + over - 4.0 * odd) + heat_odd,
        )
    cnew[...] = (0.5 * (even + odd)).reshape(BX, BY, NZ)

    spread = jnp.where(iota((NZ, 2 * NZ), 1) // 2 == iota((NZ, 2 * NZ), 0), 1.0, 0.0).astype(BF16)
    cell = iota((SLOTS, 2 * NZ), 1)
    cell_f = cell.astype(F32)
    dims = (((1,), (0,)), ((), ()))

    def advance(peer):
        got = land[peer]
        high, low = split(got)
        wide = lax.dot_general(high, spread, dims, preferred_element_type=F32)
        wide = wide + lax.dot_general(low, spread, dims, preferred_element_type=F32)
        rate = R_FINE * wide[COND_AT:COND_AT + SLOTS]
        row = jnp.broadcast_to(got[SCAL_AT:SCAL_AT + 1], (SLOTS, NZ))
        at, of = iota((SLOTS, NZ), 1), iota((SLOTS, NZ), 0)

        def scalar(i):
            return jnp.sum(jnp.where(at == of + 8 * i, row, 0.0), axis=1, keepdims=True)

        power, start, depth, named = (scalar(i) for i in range(4))
        source = jnp.where((cell_f >= start) & (cell_f < start + depth), power, 0.0)
        named = jnp.broadcast_to(named, (SLOTS, NZ)) > 0.5
        base_row = peer * (8 * SLOTS)

        def read(ref, ab):
            return jnp.concatenate(
                [ref[pl.ds(base_row + 4 * half + ab, SLOTS, stride=8), :] for half in range(2)], axis=1
            )

        temp = [read(ft, ab) for ab in range(4)]
        strain = [read(fs, ab) for ab in range(4)]
        for step in range(2):
            at = GHOST_AT + 3 * SLOTS * step
            base, along_x, along_y = (wide[at + SLOTS * i:at + SLOTS * (i + 1)] for i in range(3))
            ghosts = (base, base + along_y, base + along_x, base + along_x + along_y)
            after = []
            for ab in range(4):
                mine = temp[ab]
                beside = temp[ab ^ 2] + temp[ab ^ 1] + ghosts[ab]
                beside = beside + jnp.where(cell == 0, 0.0, pltpu.roll(mine, 1, 1))
                beside = beside + jnp.where(cell == 2 * NZ - 1, 0.0, pltpu.roll(mine, 2 * NZ - 1, 1))
                after.append(mine + rate * (beside - 6.0 * mine) + source)
            temp = after
            for ab in range(4):
                stress = (1.0 - temp[ab]) - strain[ab]
                limit = YIELD_BASE * jnp.maximum(1.0 - temp[ab] * (1.0 / MELT_TEMP), YIELD_FLOOR)
                strain[ab] = strain[ab] + (stress - jnp.clip(stress, -limit, limit))
        for ab in range(4):
            for half in range(2):
                rows = pl.ds(base_row + 4 * half + ab, SLOTS, stride=8)
                tout[rows, :] = jnp.where(named, temp[ab][:, half * NZ:(half + 1) * NZ], 0.0)
                sout[rows, :] = jnp.where(named, strain[ab][:, half * NZ:(half + 1) * NZ], 0.0)

    own_rest.wait()
    loads[7].wait()

    def take_rest(turn, carry):
        for i in range(X_CHIPS):
            step = turn * X_CHIPS + i

            @pl.when(step > 0)
            def _():
                peer = origin(step)
                message(peer, peer, FIRST, MSG - FIRST, bsend, brecv).wait_recv()

        for i in range(X_CHIPS):
            advance(origin(turn * X_CHIPS + i))
        return carry

    lax.fori_loop(0, Z_CHIPS, take_rest, 0)

    def sent(step, carry):
        peer = target(step)
        message(peer, dev, 0, FIRST, asend, arecv).wait_send()
        message(peer, dev, FIRST, MSG - FIRST, bsend, brecv).wait_send()
        return carry

    lax.fori_loop(1, DEVS, sent, 0)
    for copy in halos:
        copy.wait_send()


def to_tiles(fine):
    return fine.reshape(COLS, 4, 2, NZ).transpose(0, 2, 1, 3).reshape(COLS * 8, NZ)


def from_tiles(tiles, shape):
    return tiles.reshape(COLS, 2, 4, NZ).transpose(0, 2, 1, 3).reshape(shape)


def finish(cin, tin, sin, cout, tout, sout, sem):
    copies = [
        pltpu.make_async_copy(src, dst, sem.at[i])
        for i, (src, dst) in enumerate(((tin, tout), (sin, sout), (cin, cout)))
    ]
    for copy in copies:
        copy.start()
    for copy in copies:
        copy.wait()


def local(coarse_temp, coarse_cond, routes, track_start, track_depth, power, fine_temp, fine_strain):
    hbm = pl.BlockSpec(memory_space=pltpu.HBM)
    dma = pltpu.SemaphoreType.DMA
    shapes = ((BX, BY, NZ), (COLS * 8, NZ), (COLS * 8, NZ))
    vmem = pl.BlockSpec(memory_space=pltpu.VMEM)
    held = pl.pallas_call(
        kernel,
        out_shape=tuple(pltpu.VMEM(shape, F32) for shape in shapes),
        in_specs=[hbm] * 8,
        out_specs=(vmem,) * 3,
        scratch_shapes=[
            pltpu.VMEM((BX, BY), F32),
            pltpu.VMEM((BX, BY), jnp.int32),
            pltpu.VMEM((BX, BY), jnp.int32),
            pltpu.VMEM((BX, 1, BY), jnp.int32),
            pltpu.VMEM((BX, BY, NZ), F32),
            pltpu.VMEM((BX, BY, NZ), F32),
            pltpu.VMEM((COLS * 8, NZ), F32),
            pltpu.VMEM((COLS * 8, NZ), F32),
            pltpu.VMEM((DEVS * MSG, NZ), F32),
            pltpu.VMEM((DEVS, MSG, NZ), F32),
            pltpu.VMEM((2, 24, NZ), F32),
            pltpu.VMEM((2, 24, NZ), F32),
            pltpu.VMEM((2, 48, NZ), F32),
            pltpu.VMEM((2, 48, NZ), F32),
            pltpu.VMEM((4, 8, NZ), F32),
            pltpu.VMEM((4, 8, NZ), F32),
            pltpu.VMEM((BX + 4, 32, NZ), F32),
            pltpu.VMEM((BX + 2, 32, NZ), F32),
            pltpu.VMEM((BX + 2, 32, NZ), F32),
            pltpu.VMEM((ROWS, 6 * NZ), F32),
            pltpu.VMEM((2, ROWS, NZ), F32),
            dma((8,)),
            dma((8,)),
            dma((DEVS,)),
            dma((DEVS,)),
            dma((DEVS,)),
            dma((DEVS,)),
            dma,
            dma((8,)),
        ],
        compiler_params=pltpu.CompilerParams(
            collective_id=1, has_side_effects=True, vmem_limit_bytes=VMEM_BYTES
        ),
        name="amr_step",
    )(
        *(
            pltpu.with_memory_space_constraint(value, pltpu.HBM)
            for value in (
                power.reshape(BX, BY),
                track_start.reshape(BX, BY),
                track_depth.reshape(BX, BY),
                routes.reshape(BX, 1, BY),
                coarse_temp,
                coarse_cond,
                to_tiles(fine_temp),
                to_tiles(fine_strain),
            )
        )
    )
    cnew, tout, sout = pl.pallas_call(
        finish,
        out_shape=tuple(pltpu.HBM(shape, F32) for shape in shapes),
        in_specs=[vmem] * 3,
        out_specs=(hbm,) * 3,
        scratch_shapes=[dma((3,))],
        name="write_results",
    )(*(pltpu.with_memory_space_constraint(value, pltpu.VMEM) for value in held))
    return cnew, from_tiles(tout, fine_temp.shape), from_tiles(sout, fine_strain.shape)


def solution(mesh):
    placed = (
        P("group", "dev", None),
        P("group", "dev", None),
        P("group", "dev", None, None, None),
        P("group", "dev", None, None),
        P("group", "dev", None, None),
        P("group", "dev", None, None),
        P("group", "dev", None, None, None, None),
        P("group", "dev", None, None, None, None),
    )
    return jax.shard_map(
        local,
        mesh=mesh,
        in_specs=placed,
        out_specs=(
            P("group", "dev", None),
            P("group", "dev", None, None, None, None),
            P("group", "dev", None, None, None, None),
        ),
        check_vma=False,
    )
```

```python
import functools

import jax
import jax.numpy as jnp
from jax import lax
from jax.experimental import pallas as pl
from jax.experimental.pallas import tpu as pltpu
from jax.sharding import PartitionSpec as P

R_COARSE = 0.08
R_FINE = 0.16
YIELD_BASE = 0.6
MELT_TEMP = 3.0
YIELD_FLOOR = 0.05

MESH = pl.DeviceIdType.MESH
VMEM_BYTES = 40 * 2**20
F32 = jnp.float32
BF16 = jnp.bfloat16

X_CHIPS, Z_CHIPS = 4, 8
DEVS = X_CHIPS * Z_CHIPS
SLOTS = 6
COLS = DEVS * SLOTS
BX, BY, NZ = 8, 16, 128
ROWS = BX * BY

MEAN_AT = 0
COND_AT = 12
SCAL_AT = 18
GHOST_AT = 20
FIRST = 16
MSG = 56

CORNERS = ((1, 1), (1, -1), (-1, 1), (-1, -1))


def offset_of(step):
    away = (step + X_CHIPS) // (2 * X_CHIPS)
    turn = (step + X_CHIPS) % (2 * X_CHIPS)
    middle = (away == 0) | (away == Z_CHIPS // 2)
    ox = jnp.where(middle, step % X_CHIPS, turn // 2)
    return ox, jnp.where(middle, away, away * (1 - 2 * (turn % 2)))


def turn_of(z):
    return jnp.where(z < 6, z, 13 - z)


def split(value):
    high = value.astype(BF16)
    return high, (value - high.astype(F32)).astype(BF16)


def pick(chooser, value, dims=((1,), (0,))):
    total = None
    for part in split(value):
        term = lax.dot_general(chooser, part, (dims, ((), ())), preferred_element_type=F32)
        total = term if total is None else total + term
    return total


def iota(shape, dim):
    return lax.broadcasted_iota(jnp.int32, shape, dim)


def kernel(
    power_in, start_in, depth_in, routes_in, ct_in, cc_in, ft_in, fs_in, cnew, tout, sout,
        power_v, start_v, depth_v, routes_v, ct, cc, ft, fs, outb, land, hys, hyl, hxs, hxl, hcs, hcl, oe, ce, me, field, side,
    hsend, hrecv, asend, arecv, bsend, brecv, lsem, isem,
):
    group = lax.axis_index("group")
    groups = lax.axis_size("group")
    dev = lax.axis_index("dev")
    dx, dz = dev // Z_CHIPS, dev % Z_CHIPS

    def target(step):
        ox, oz = offset_of(step)
        return ((dx + ox) % X_CHIPS) * Z_CHIPS + (dz + oz + Z_CHIPS) % Z_CHIPS

    def origin(step):
        ox, oz = offset_of(step)
        return ((dx - ox + X_CHIPS) % X_CHIPS) * Z_CHIPS + (dz - oz + Z_CHIPS) % Z_CHIPS

    def near(dg, dd):
        return {"group": (group + dg + groups) % groups, "dev": (dev + dd + DEVS) % DEVS}

    barrier = pltpu.get_barrier_semaphore()

    def greet(step, carry):
        pl.semaphore_signal(barrier, inc=1, device_id={"dev": target(step)}, device_id_type=MESH)
        return carry

    lax.fori_loop(1, DEVS, greet, 0)
    for dg, dd in ((1, 0), (-1, 0)) + CORNERS:
        pl.semaphore_signal(barrier, inc=1, device_id=near(dg, dd), device_id_type=MESH)

    loads = []
    arrays = ((routes_in, routes_v), (power_in, power_v), (start_in, start_v), (depth_in, depth_v))
    arrays = arrays + ((ct_in, ct), (cc_in, cc), (ft_in, ft), (fs_in, fs))
    for i, (src, dst) in enumerate(arrays):
        load = pltpu.make_async_copy(src, dst, isem.at[i])
        load.start()
        loads.append(load)
    for load in loads[:6]:
        load.wait()

    for x in range(BX):
        hys[0, 2 * x:2 * x + 2] = ct[x, BY - 2:BY]
        hys[0, 16 + x:17 + x] = cc[x, BY - 1:BY]
        hys[1, 2 * x:2 * x + 2] = ct[x, 0:2]
        hys[1, 16 + x:17 + x] = cc[x, 0:1]
    for i, (lo, edge) in enumerate(((BX - 2, BX - 1), (0, 0))):
        hxs[i, 0:16] = ct[lo]
        hxs[i, 16:32] = ct[lo + 1]
        hxs[i, 32:48] = cc[edge]
    for i, (dg, dd) in enumerate(CORNERS):
        row = BX - 1 if dg > 0 else 0
        hcs[i] = jnp.broadcast_to(ct[row, BY - 1:BY] if dd > 0 else ct[row, 0:1], (8, NZ))

    held = [power_v[...], start_v[...].astype(F32), depth_v[...].astype(F32), routes_v[:, 0, :].astype(F32)]
    same_y = jnp.where(iota((BY, ROWS), 1) % BY == iota((BY, ROWS), 0), 1.0, 0.0).astype(BF16)
    dims = (((1,), (0,)), ((), ()))
    flat = None
    for part in split(jnp.concatenate(held, axis=0)):
        term = lax.dot_general(part, same_y, dims, preferred_element_type=F32)
        flat = term if flat is None else flat + term
    same_x = iota((4 * BX, ROWS), 1) // BY == iota((4 * BX, ROWS), 0) % BX
    flat = jnp.where(same_x, flat, 0.0)
    power, start, depth, owner = (jnp.sum(flat[BX * i:BX * (i + 1)], axis=0, keepdims=True) for i in range(4))
    owner_b = jnp.broadcast_to(owner, (DEVS, ROWS))
    hot = jnp.where(owner_b == iota((DEVS, ROWS), 0).astype(F32), 1.0, 0.0)
    earlier = jnp.where(iota((ROWS, ROWS), 0) < iota((ROWS, ROWS), 1), 1.0, 0.0).astype(BF16)
    before = lax.dot_general(hot.astype(BF16), earlier, (((1,), (0,)), ((), ())), preferred_element_type=F32)
    slot = jnp.sum(before * hot, axis=0, keepdims=True)
    code = slot * DEVS + owner
    to_slot = jnp.where(jnp.broadcast_to(code, (COLS, ROWS)) == iota((COLS, ROWS), 0).astype(F32), 1.0, 0.0).astype(BF16)
    code_t = jnp.transpose(jnp.broadcast_to(code, (ROWS, ROWS)))
    start_t = jnp.transpose(jnp.broadcast_to(start, (ROWS, ROWS)))
    depth_t = jnp.transpose(jnp.broadcast_to(depth, (ROWS, ROWS)))
    power_t = jnp.transpose(jnp.broadcast_to(power, (ROWS, ROWS)))
    lanes = iota((ROWS, ROWS), 1).astype(F32)
    from_slot = jnp.concatenate(
        [jnp.where(code_t == lanes, 1.0, 0.0), jnp.where(code_t == lanes + ROWS, 1.0, 0.0)], axis=1
    ).astype(BF16)

    conds = pick(to_slot, cc[...].reshape(ROWS, NZ))
    for k in range(SLOTS):
        outb[pl.ds(COND_AT + k, DEVS, stride=MSG), :] = conds[k * DEVS:(k + 1) * DEVS]
    at_slot = jnp.broadcast_to(slot, (8, ROWS)) == iota((8, ROWS), 0).astype(F32)
    blocks = [jnp.where(at_slot, jnp.broadcast_to(v, (8, ROWS)), 0.0) for v in (power, start, depth)]
    blocks = blocks + [jnp.where(at_slot, 1.0, 0.0), jnp.zeros((NZ - 32, ROWS), F32)]
    scalars = pick(hot.astype(BF16), jnp.concatenate(blocks, axis=0), ((1,), (1,)))
    outb[pl.ds(SCAL_AT, DEVS, stride=MSG), :] = scalars
    outb[pl.ds(SCAL_AT + 1, DEVS, stride=MSG), :] = jnp.zeros_like(scalars)

    loads[6].wait()
    for k in range(SLOTS):
        for half in range(2):
            total = None
            for ab in range(4):
                term = ft[pl.ds(8 * k + 4 * half + ab, DEVS, stride=8 * SLOTS), :]
                total = term if total is None else total + term
            outb[pl.ds(MEAN_AT + SLOTS * half + k, DEVS, stride=MSG), :] = 0.25 * total

    oe[...] = jnp.zeros_like(oe)
    ce[...] = jnp.zeros_like(ce)
    for x in range(BX):
        oe[2 + x, 8:24] = ct[x]
        ce[1 + x, 8:24] = cc[x]

    def own(lo, n):
        src = outb.at[pl.ds(pl.multiple_of(dev * MSG + lo, 8), n)]
        return pltpu.make_async_copy(src, land.at[dev, pl.ds(lo, n)], lsem)

    def message(peer, sender, lo, n, send, recv):
        src = outb.at[pl.ds(pl.multiple_of(peer * MSG + lo, 8), n)]
        return pltpu.make_async_remote_copy(
            src, land.at[sender, pl.ds(lo, n)], send.at[peer], recv.at[sender],
            device_id={"dev": peer}, device_id_type=MESH,
        )

    pl.semaphore_wait(barrier, DEVS - 1 + 2 + len(CORNERS))

    halos = []
    plan = [(hys, hyl, 0, 0, 1), (hys, hyl, 1, 0, -1), (hxs, hxl, 0, 1, 0), (hxs, hxl, 1, -1, 0)]
    plan = plan + [(hcs, hcl, i, dg, dd) for i, (dg, dd) in enumerate(CORNERS)]
    for number, (src, dst, i, dg, dd) in enumerate(plan):
        copy = pltpu.make_async_remote_copy(
            src.at[i], dst.at[i], hsend.at[number], hrecv.at[number],
            device_id=near(dg, dd), device_id_type=MESH,
        )
        copy.start()
        halos.append(copy)

    def send_first(step, carry):
        message(target(step), dev, 0, FIRST, asend, arecv).start()
        return carry

    def first_by_turn(i, carry):
        peer = (dx + i) % X_CHIPS * Z_CHIPS + turn_of(i // X_CHIPS)

        @pl.when(peer != dev)
        def _():
            message(peer, dev, 0, FIRST, asend, arecv).start()

        return carry

    lax.fori_loop(0, DEVS, first_by_turn, 0)
    own_first = own(0, FIRST)
    own_first.start()

    for copy in halos:
        copy.wait_recv()

    low_x, high_x = group > 0, group < groups - 1
    low_y, high_y = dev > 0, dev < DEVS - 1

    def inside(ok, value):
        return jnp.where(ok, value, 0.0)

    for x in range(BX):
        oe[2 + x, 6:8] = inside(low_y, hyl[0, 2 * x:2 * x + 2])
        oe[2 + x, 24:26] = inside(high_y, hyl[1, 2 * x:2 * x + 2])
        ce[1 + x, 7:8] = inside(low_y, hyl[0, 16 + x:17 + x])
        ce[1 + x, 24:25] = inside(high_y, hyl[1, 16 + x:17 + x])
    oe[0, 8:24] = inside(low_x, hxl[0, 0:16])
    oe[1, 8:24] = inside(low_x, hxl[0, 16:32])
    ce[0, 8:24] = inside(low_x, hxl[0, 32:48])
    oe[BX + 2, 8:24] = inside(high_x, hxl[1, 0:16])
    oe[BX + 3, 8:24] = inside(high_x, hxl[1, 16:32])
    ce[BX + 1, 8:24] = inside(high_x, hxl[1, 32:48])
    oe[1, 7:8] = inside(low_x & low_y, hcl[0, 0:1])
    oe[1, 24:25] = inside(low_x & high_y, hcl[1, 0:1])
    oe[BX + 2, 7:8] = inside(high_x & low_y, hcl[2, 0:1])
    oe[BX + 2, 24:25] = inside(high_x & high_y, hcl[3, 0:1])

    lane = iota((32, NZ), 1)
    for x in range(BX + 2):
        cur = oe[x + 1]
        beside = oe[x] + oe[x + 2] + pltpu.roll(cur, 1, 0) + pltpu.roll(cur, 31, 0)
        beside = beside + jnp.where(lane == 0, 0.0, pltpu.roll(cur, 1, 1))
        beside = beside + jnp.where(lane == NZ - 1, 0.0, pltpu.roll(cur, NZ - 1, 1))
        new = cur + R_COARSE * ce[x] * (beside - 6.0 * cur)
        me[x] = 0.5 * (cur + new)

    for x in range(BX):
        for step, (arr, at) in enumerate(((oe, x + 2), (me, x + 1))):
            west, east = arr[at - 1, 8:24], arr[at + 1, 8:24]
            south, north = arr[at, 7:23], arr[at, 9:25]
            base, along_x, along_y = west + south, east - west, north - south
            for i, value in enumerate((base, along_x, along_y)):
                f = 3 * step + i
                field[x * BY:(x + 1) * BY, f * NZ:(f + 1) * NZ] = value
            side[step, x * BY:(x + 1) * BY] = base + 0.5 * (along_x + along_y)

    ghosts = pick(to_slot, field[...])
    for f in range(6):
        for k in range(SLOTS):
            outb[pl.ds(GHOST_AT + SLOTS * f + k, DEVS, stride=MSG), :] = ghosts[k * DEVS:(k + 1) * DEVS, f * NZ:(f + 1) * NZ]

    def send_rest(step, carry):
        message(target(step), dev, FIRST, MSG - FIRST, bsend, brecv).start()
        return carry

    def by_turn(i, carry):
        peer = (dx + i) % X_CHIPS * Z_CHIPS + turn_of(i // X_CHIPS)

        @pl.when(peer != dev)
        def _():
            message(peer, dev, FIRST, 24, bsend, brecv).start()
            message(peer, dev, FIRST + 24, 16, bsend, brecv).start()

        return carry

    lax.fori_loop(0, DEVS, by_turn, 0)
    own_first.wait()
    own_rest = own(FIRST, MSG - FIRST)
    own_rest.start()

    def take_first(step, carry):
        message(origin(step), origin(step), 0, FIRST, asend, arecv).wait_recv()
        return carry

    lax.fori_loop(1, DEVS, take_first, 0)
    halves = []
    for half in range(2):
        rows = [land[:, MEAN_AT + SLOTS * half + k, :] for k in range(SLOTS)] + [jnp.zeros((2 * ROWS - COLS, NZ), F32)]
        halves.append(jnp.concatenate(rows, axis=0))
    fine = pick(from_slot, jnp.concatenate(halves, axis=1))
    row_i, col_i = iota((2 * NZ, 2 * NZ), 0), iota((2 * NZ, 2 * NZ), 1)
    wanted = jnp.where(col_i < NZ, 2 * col_i, 2 * (col_i - NZ) + 1)
    high, low = split(fine)
    apart = jnp.where(row_i == wanted, 1.0, 0.0).astype(BF16)
    dims = (((1,), (0,)), ((), ()))
    both = lax.dot_general(high, apart, dims, preferred_element_type=F32)
    both = both + lax.dot_general(low, apart, dims, preferred_element_type=F32)
    even, odd = both[:, :NZ], both[:, NZ:]
    rate = R_FINE * cc[...].reshape(ROWS, NZ)
    place = iota((ROWS, NZ), 1)

    def heat(fine_cell):
        cell = fine_cell.astype(F32)
        return jnp.where((cell >= start_t) & (cell < start_t + depth_t), power_t, 0.0)

    heat_even, heat_odd = heat(2 * place), heat(2 * place + 1)
    for step in range(2):
        under = jnp.where(place == 0, 0.0, pltpu.roll(odd, 1, 1))
        over = jnp.where(place == NZ - 1, 0.0, pltpu.roll(even, NZ - 1, 1))
        ghost = side[step]
        even, odd = (
            even + rate * (ghost + odd + under - 4.0 * even) + heat_even,
            odd + rate * (ghost + even + over - 4.0 * odd) + heat_odd,
        )
    cnew[...] = (0.5 * (even + odd)).reshape(BX, BY, NZ)

    spread = jnp.where(iota((NZ, 2 * NZ), 1) // 2 == iota((NZ, 2 * NZ), 0), 1.0, 0.0).astype(BF16)
    cell = iota((SLOTS, 2 * NZ), 1)
    cell_f = cell.astype(F32)
    dims = (((1,), (0,)), ((), ()))

    def advance(peer):
        got = land[peer]
        high, low = split(got)
        wide = lax.dot_general(high, spread, dims, preferred_element_type=F32)
        wide = wide + lax.dot_general(low, spread, dims, preferred_element_type=F32)
        rate = R_FINE * wide[COND_AT:COND_AT + SLOTS]
        row = jnp.broadcast_to(got[SCAL_AT:SCAL_AT + 1], (SLOTS, NZ))
        at, of = iota((SLOTS, NZ), 1), iota((SLOTS, NZ), 0)

        def scalar(i):
            return jnp.sum(jnp.where(at == of + 8 * i, row, 0.0), axis=1, keepdims=True)

        power, start, depth, named = (scalar(i) for i in range(4))
        source = jnp.where((cell_f >= start) & (cell_f < start + depth), power, 0.0)
        named = jnp.broadcast_to(named, (SLOTS, NZ)) > 0.5
        base_row = peer * (8 * SLOTS)

        def read(ref, ab):
            return jnp.concatenate(
                [ref[pl.ds(base_row + 4 * half + ab, SLOTS, stride=8), :] for half in range(2)], axis=1
            )

        temp = [read(ft, ab) for ab in range(4)]
        strain = [read(fs, ab) for ab in range(4)]
        for step in range(2):
            at = GHOST_AT + 3 * SLOTS * step
            base, along_x, along_y = (wide[at + SLOTS * i:at + SLOTS * (i + 1)] for i in range(3))
            ghosts = (base, base + along_y, base + along_x, base + along_x + along_y)
            after = []
            for ab in range(4):
                mine = temp[ab]
                beside = temp[ab ^ 2] + temp[ab ^ 1] + ghosts[ab]
                beside = beside + jnp.where(cell == 0, 0.0, pltpu.roll(mine, 1, 1))
                beside = beside + jnp.where(cell == 2 * NZ - 1, 0.0, pltpu.roll(mine, 2 * NZ - 1, 1))
                after.append(mine + rate * (beside - 6.0 * mine) + source)
            temp = after
            for ab in range(4):
                stress = (1.0 - temp[ab]) - strain[ab]
                limit = YIELD_BASE * jnp.maximum(1.0 - temp[ab] * (1.0 / MELT_TEMP), YIELD_FLOOR)
                strain[ab] = strain[ab] + (stress - jnp.clip(stress, -limit, limit))
        for ab in range(4):
            for half in range(2):
                rows = pl.ds(base_row + 4 * half + ab, SLOTS, stride=8)
                tout[rows, :] = jnp.where(named, temp[ab][:, half * NZ:(half + 1) * NZ], 0.0)
                sout[rows, :] = jnp.where(named, strain[ab][:, half * NZ:(half + 1) * NZ], 0.0)

    own_rest.wait()
    loads[7].wait()

    def take_rest(turn, carry):
        z = turn_of(turn)
        for x in range(X_CHIPS):
            peer = x * Z_CHIPS + z

            @pl.when(peer != dev)
            def _():
                message(peer, peer, FIRST, MSG - FIRST, bsend, brecv).wait_recv()

        for x in range(X_CHIPS):
            advance(x * Z_CHIPS + z)
        return carry

    lax.fori_loop(0, Z_CHIPS, take_rest, 0)

    def sent(step, carry):
        peer = target(step)
        message(peer, dev, 0, FIRST, asend, arecv).wait_send()
        message(peer, dev, FIRST, MSG - FIRST, bsend, brecv).wait_send()
        return carry

    lax.fori_loop(1, DEVS, sent, 0)
    for copy in halos:
        copy.wait_send()


def to_tiles(fine):
    return fine.reshape(COLS, 4, 2, NZ).transpose(0, 2, 1, 3).reshape(COLS * 8, NZ)


def from_tiles(tiles, shape):
    return tiles.reshape(COLS, 2, 4, NZ).transpose(0, 2, 1, 3).reshape(shape)


def finish(cin, tin, sin, cout, tout, sout, sem):
    copies = [
        pltpu.make_async_copy(src, dst, sem.at[i])
        for i, (src, dst) in enumerate(((tin, tout), (sin, sout), (cin, cout)))
    ]
    for copy in copies:
        copy.start()
    for copy in copies:
        copy.wait()


def local(coarse_temp, coarse_cond, routes, track_start, track_depth, power, fine_temp, fine_strain):
    hbm = pl.BlockSpec(memory_space=pltpu.HBM)
    dma = pltpu.SemaphoreType.DMA
    shapes = ((BX, BY, NZ), (COLS * 8, NZ), (COLS * 8, NZ))
    vmem = pl.BlockSpec(memory_space=pltpu.VMEM)
    held = pl.pallas_call(
        kernel,
        out_shape=tuple(pltpu.VMEM(shape, F32) for shape in shapes),
        in_specs=[hbm] * 8,
        out_specs=(vmem,) * 3,
        scratch_shapes=[
            pltpu.VMEM((BX, BY), F32),
            pltpu.VMEM((BX, BY), jnp.int32),
            pltpu.VMEM((BX, BY), jnp.int32),
            pltpu.VMEM((BX, 1, BY), jnp.int32),
            pltpu.VMEM((BX, BY, NZ), F32),
            pltpu.VMEM((BX, BY, NZ), F32),
            pltpu.VMEM((COLS * 8, NZ), F32),
            pltpu.VMEM((COLS * 8, NZ), F32),
            pltpu.VMEM((DEVS * MSG, NZ), F32),
            pltpu.VMEM((DEVS, MSG, NZ), F32),
            pltpu.VMEM((2, 24, NZ), F32),
            pltpu.VMEM((2, 24, NZ), F32),
            pltpu.VMEM((2, 48, NZ), F32),
            pltpu.VMEM((2, 48, NZ), F32),
            pltpu.VMEM((4, 8, NZ), F32),
            pltpu.VMEM((4, 8, NZ), F32),
            pltpu.VMEM((BX + 4, 32, NZ), F32),
            pltpu.VMEM((BX + 2, 32, NZ), F32),
            pltpu.VMEM((BX + 2, 32, NZ), F32),
            pltpu.VMEM((ROWS, 6 * NZ), F32),
            pltpu.VMEM((2, ROWS, NZ), F32),
            dma((8,)),
            dma((8,)),
            dma((DEVS,)),
            dma((DEVS,)),
            dma((DEVS,)),
            dma((DEVS,)),
            dma,
            dma((8,)),
        ],
        compiler_params=pltpu.CompilerParams(
            collective_id=1, has_side_effects=True, vmem_limit_bytes=VMEM_BYTES
        ),
        name="amr_step",
    )(
        *(
            pltpu.with_memory_space_constraint(value, pltpu.HBM)
            for value in (
                power.reshape(BX, BY),
                track_start.reshape(BX, BY),
                track_depth.reshape(BX, BY),
                routes.reshape(BX, 1, BY),
                coarse_temp,
                coarse_cond,
                to_tiles(fine_temp),
                to_tiles(fine_strain),
            )
        )
    )
    cnew, tout, sout = pl.pallas_call(
        finish,
        out_shape=tuple(pltpu.HBM(shape, F32) for shape in shapes),
        in_specs=[vmem] * 3,
        out_specs=(hbm,) * 3,
        scratch_shapes=[dma((3,))],
        name="write_results",
    )(*(pltpu.with_memory_space_constraint(value, pltpu.VMEM) for value in held))
    return cnew, from_tiles(tout, fine_temp.shape), from_tiles(sout, fine_strain.shape)


def solution(mesh):
    placed = (
        P("group", "dev", None),
        P("group", "dev", None),
        P("group", "dev", None, None, None),
        P("group", "dev", None, None),
        P("group", "dev", None, None),
        P("group", "dev", None, None),
        P("group", "dev", None, None, None, None),
        P("group", "dev", None, None, None, None),
    )
    return jax.shard_map(
        local,
        mesh=mesh,
        in_specs=placed,
        out_specs=(
            P("group", "dev", None),
            P("group", "dev", None, None, None, None),
            P("group", "dev", None, None, None, None),
        ),
        check_vma=False,
    )
```
